128 devices in a mesh: row: 32 (over x, z, core), col: 4 (over y).
Axes of the slice: x: 4, y: 4, z: 4, core: 2. Of those that a mesh axis runs over, the one named last changes fastest.
Arguments:
- front: float32 [6, 32, 128, 16, 4, 128], P(None, 'row', None, None, 'col'), may hold values from -6 to 6
- mask: int32 [6, 32, 16, 4], P(None, 'row', None, 'col'), may hold values 0 or 1
- child_tiles: float32 [24576, 16384], P(('row', 'col')), may hold values from -6 to 6
- owner_map: int32 [24576, 1], P(('row', 'col')), may hold values from 0 to 127; in each aligned block of 192 rows (0 to 191, 192 to 383, ...) at most 2 rows name the same one
- parent_slot: int32 [24576], P(('row', 'col')), may hold values from 0 to 95
- pivot_order: int32 [512], replicated, may hold values from 0 to 511, each once
- inv_pivot: float32 [512, 512], replicated, as said below
Outputs:
- updated_front: float32 [6, 32, 128, 16, 4, 128], P(None, 'row', None, None, 'col')
The draws below stay inside these ranges and needn't reach their ends.
Inputs may be any that keep to these rules, and one draw needn't show every extreme that they name: owner_map[t, 0] is the device r * 4 + c whose blocks receive tile t; among the 192 tiles of one device at most 2 name the same device, and exactly 2 do for some. parent_slot[t] is a 16 + b for the receiving device's local block (a, b). inv_pivot is symmetric.
All inputs are finite; a program needn't handle non-finite values. No bound on the sum of `mask` on one device may be relied on, other than what follows from the above.
Results may differ from the reference program's by a relative error of at most 0.00009.
Values sent between devices are 32-bit elements; how exact they have to be, the bound alone decides.
A program may use at most 192 MiB of HBM per device.

```python
import math
import jax
import jax.numpy as jnp
import numpy as np
from jax import lax

BLK = 128
FRONT = 24576
PB = 4
MOST = 2
BLK_COLS = 16
PANEL = 512
BLK_ROWS = 6
WIN = 8192
TILES_DEV = 192
TILES = 24576
N_ROW = 32
N_COL = 4


def draw_inv_pivot(key, part):
    key = jax.random.fold_in(key, 7)
    key_diag, key_off = jax.random.split(key)
    diag_part = jax.random.uniform(key_diag, (PANEL,), jnp.float32, 0.5, 1.5)
    normal_part = jax.random.normal(key_off, (PANEL, PANEL), jnp.float32)
    symmetric = (normal_part + normal_part.T) * (0.4 / math.sqrt(2.0 * PANEL))
    identity = (jnp.arange(PANEL)[:, None] == jnp.arange(PANEL)[None, :]).astype(jnp.float32)
    return 0.05 * (identity * diag_part[:, None] + symmetric)


def set_ends(array, key, low, largest):
    spot = [jax.random.randint(jax.random.fold_in(key, axis), (), 0, length) for axis, length in enumerate(array.shape)]
    widest = array.shape.index(max(array.shape))
    next_to = spot[:widest] + [(spot[widest] + 1) % array.shape[widest]] + spot[widest + 1:]
    return array.at[tuple(spot)].set(low).at[tuple(next_to)].set(largest)


def level_of(key, shape, cuts, least, high):
    def one(axis_at, parts):
        draws = jax.random.uniform(jax.random.fold_in(jax.random.fold_in(key, 6), axis_at), (parts,), jnp.float32, least / len(cuts), high / len(cuts))
        return jnp.repeat(jnp.exp(draws), shape[axis_at] // parts).reshape((-1,) + (1,) * (len(shape) - axis_at - 1))

    loudness = one(*cuts[0])
    for cut in cuts[1:]:
        loudness = loudness * one(*cut)
    return loudness


def deal_out(stream_key, own, number, rows, amount, top, limit, skew):
    order = jax.random.permutation(stream_key, amount)
    heavy_load, common = shares(amount, rows * top, limit, skew, True), shares(amount, rows * top, limit, skew, False)
    places = jnp.arange(amount)

    def named(lengths, rotation):
        used = int((lengths > 0).sum())
        fixed = max(1, used // 4)
        shifted = fixed + (places - fixed + rotation * (used - fixed)) % max(1, amount - fixed)
        return jnp.zeros((amount,), jnp.int32).at[order[jnp.where(places < fixed, places, shifted)]].set(jnp.asarray(lengths, jnp.int32))

    lengths = jnp.where(number % 4 == 0, named(heavy_load, number // 4), named(common, number - number // 4 - 1))
    mixed = jax.random.permutation(jax.random.fold_in(own, 3), amount)
    source_of, receiver = mixed[0:amount // 2 * 2:2], mixed[1:amount // 2 * 2:2]
    margin = jnp.minimum(lengths[source_of] - 1, limit - lengths[receiver]) // 2
    margin = jnp.where((source_of == order[0]) | (receiver == order[0]) | (lengths[receiver] == 0), 0, jnp.maximum(margin, 0))
    shifted = jax.random.randint(jax.random.fold_in(own, 4), (amount // 2,), 0, 1 << 20) % (margin + 1)
    lengths = lengths.at[source_of].add(-shifted).at[receiver].add(shifted)
    items = jnp.searchsorted(jnp.cumsum(lengths), jnp.arange(rows * top), side="right").astype(jnp.int32)
    grid = items.reshape(top, rows).T
    grid = grid[jax.random.permutation(jax.random.fold_in(own, 1), rows)]
    rotation = jax.random.randint(jax.random.fold_in(own, 2), (rows, 1), 0, top)
    return jnp.take_along_axis(grid, (jnp.arange(top)[None, :] + rotation) % top, axis=1)


def shares(number_of, total, reach, skew, full):
    weights = [(1 << 20) // math.isqrt(standing ** skew) + 1 for standing in range(1, number_of + 1)]
    largest = reach if full else min(reach, max(-(-total // number_of), total * weights[0] // sum(weights)))
    least = 1 if total - largest >= number_of - 1 else 0
    given, spare = [largest] + [least] * (number_of - 1), total - largest - least * (number_of - 1)
    while spare > 0:
        movable = [i for i in range(1, number_of) if given[i] < largest] or [i for i in range(1, number_of) if given[i] < reach]
        pool, left = sum([weights[i] for i in movable]), spare
        for i in movable:
            extra = min(reach - given[i], max(1, left * weights[i] // pool), spare)
            given[i] = given[i] + extra
            spare = spare - extra
    return np.array(given)


def noise(rng, dims, spread, reach, cuts=(), kind=jnp.bfloat16):
    values = jax.random.normal(rng, dims, jnp.float32) * spread
    if len(cuts) > 0:
        values = level_of(rng, dims, cuts, -0.22, 0.18) * values
    return jnp.clip(values, min=-reach, max=reach).astype(kind)


def setup_inputs(seed: int = 0) -> dict:
    arg_keys = jax.random.split(jax.random.key(seed), 8)
    front = noise(arg_keys[0], (BLK_ROWS, N_ROW, BLK, BLK_COLS, N_COL, BLK), 1.0, 6.0, ((1, 32), (4, 4)), jnp.float32)
    mask = set_ends((jax.random.randint(arg_keys[1], (BLK_ROWS, N_ROW, BLK_COLS, N_COL), 0, 2) < 1).astype(jnp.int32), jax.random.fold_in(arg_keys[1], 1), 0, 1)
    child_tiles = noise(arg_keys[2], (TILES, BLK * BLK), 1.0, 6.0, ((0, 128),), jnp.float32)
    owner_map_keys = jax.random.split(jax.random.fold_in(arg_keys[3], 1), TILES // TILES_DEV)
    owner_map_turns = jax.random.permutation(jax.random.fold_in(arg_keys[3], 3), TILES // TILES_DEV)
    owner_map = jax.vmap(lambda own, number: deal_out(jax.random.fold_in(arg_keys[3], 2), own, number, TILES_DEV, N_ROW * N_COL, 1, MOST, 2))(owner_map_keys, owner_map_turns).reshape((TILES, 1))
    parent_slot = set_ends(jax.random.randint(arg_keys[4], (TILES,), 0, BLK_ROWS * BLK_COLS), jax.random.fold_in(arg_keys[4], 1), 0, (BLK_ROWS * BLK_COLS) - 1).astype(jnp.int32)
    pivot_order = jax.random.permutation(arg_keys[5], PANEL).astype(jnp.int32)
    inv_pivot = draw_inv_pivot(jax.random.fold_in(arg_keys[7], 71), 0)
    return dict(front=front, mask=mask, child_tiles=child_tiles, owner_map=owner_map, parent_slot=parent_slot, pivot_order=pivot_order, inv_pivot=inv_pivot)


def reference(front, mask, child_tiles, owner_map, parent_slot, pivot_order, inv_pivot):
    owner_dev = owner_map[:, 0]
    row_owner = owner_dev // N_COL
    col_owner = owner_dev % N_COL
    row_local = parent_slot // BLK_COLS
    col_local = parent_slot % BLK_COLS
    pieces = child_tiles.reshape(-1, BLK, BLK)
    assembled = front.at[row_local, row_owner, :, col_local, col_owner, :].add(pieces)
    block_rows = BLK_ROWS * N_ROW
    block_cols = BLK_COLS * N_COL
    matrix = assembled.reshape(FRONT, WIN)
    permuted = jnp.take(matrix[:, :PANEL], pivot_order, axis=1)
    factor = jnp.dot(permuted, inv_pivot, precision=lax.Precision.HIGHEST)
    trailing = permuted[PANEL:WIN]
    keep_block = mask.reshape(block_rows, block_cols)[:, PB:] > 0

    def one_row(block_index):
        front_rows = lax.dynamic_slice_in_dim(matrix, block_index * BLK, BLK, 0)
        factor_rows = lax.dynamic_slice_in_dim(factor, block_index * BLK, BLK, 0)
        update = jnp.einsum("rp,cp->rc", factor_rows, trailing, precision=lax.Precision.HIGHEST)
        schur_part = (front_rows[:, PANEL:] - update).reshape(BLK, block_cols - PB, BLK)
        keep_flags = keep_block[block_index]
        schur_part = jnp.where(keep_flags[None, :, None], schur_part, 0.0)
        return jnp.concatenate([factor_rows, schur_part.reshape(BLK, WIN - PANEL)], 1)

    result = lax.map(one_row, jnp.arange(block_rows, dtype=jnp.int32))
    return result.reshape(front.shape)
```

```python
import functools

import jax
import jax.numpy as jnp
from jax import lax
from jax.experimental import pallas as pl
from jax.experimental.pallas import tpu as pltpu
from jax.sharding import PartitionSpec as P

MOST = 2
CAP = 48
SLOTS = 4 * CAP
MESH = pl.DeviceIdType.MESH
F32 = jnp.float32
BF16 = jnp.bfloat16
PART_CHUNKS = ((8, 12, 12, 12), (8, 12, 12, 12), (8, 8, 12, 12))
CHUNKS = []
_row = 0
for _p, _sizes in enumerate(PART_CHUNKS):
    for _k, _n in enumerate(_sizes):
        CHUNKS.append((_k, _p, _row, _n))
        _row += _n
CHUNKS.sort()
N_CHUNKS = len(CHUNKS)
AXES = ((0, 1, 2), (1, 2, 0), (2, 0, 1))


def exchange_kernel(
    child, front, owner, slot, mask_row, out, flag,
    buf, recv1, recv2, recv3, sib, fbuf, tabs, mown, mcore, mtwo, mx, mfour, mz, my,
    hsend, hrecv, fsend, frecv,
    child_sem, front_sem, out_sem, send_sem, recv_sem, sib_ssem, sib_rsem,
    m_ssem, m_rsem, h_ssem, h_rsem, f_ssem, f_rsem,
):
    row_at, y = lax.axis_index("row"), lax.axis_index("col")
    x, z, core = row_at // 8, (row_at // 2) % 4, row_at % 2

    def peer(axis, shift):
        if axis == 0:
            return (((x + shift) % 4) * 8 + z * 2 + core, y)
        if axis == 1:
            return (x * 8 + ((z + shift) % 4) * 2 + core, y)
        return (row_at, (y + shift) % 4)

    sibling = (row_at + 1 - 2 * core, y)
    here = (x, z, y)

    def remote(src, dst, ssem, rsem, to):
        return pltpu.make_async_remote_copy(
            src_ref=src, dst_ref=dst, send_sem=ssem, recv_sem=rsem, device_id=to, device_id_type=MESH
        )

    front_in = pltpu.make_async_copy(front, fbuf, front_sem)
    for n, (_, _, r0, rows) in enumerate(CHUNKS):

        def load(g, carry, n=n, r0=r0, rows=rows):
            pltpu.make_async_copy(
                child.at[g, pl.ds(r0, rows)],
                buf.at[pl.ds(r0, rows), pl.ds(pl.multiple_of(g * 8, 8), 8), :],
                child_sem.at[n],
            ).start()
            return carry

        lax.fori_loop(0, SLOTS // 8, load, 0)
    front_in.start()

    barrier = pltpu.get_barrier_semaphore()
    for axis in range(3):
        for shift in (1, 2, 3):
            pl.semaphore_signal(barrier, inc=1, device_id=peer(axis, shift), device_id_type=MESH)
    pl.semaphore_signal(barrier, inc=1, device_id=sibling, device_id_type=MESH)
    pl.semaphore_wait(barrier, 10)

    sub8 = lax.broadcasted_iota(jnp.int32, (8, 128), 0)
    mown[...] = jnp.where(sub8 == x * 2 + core, jnp.broadcast_to(mask_row[0:1, :], (8, 128)), 0.0)
    copy = remote(mown, mcore, m_ssem.at[0], m_rsem.at[0], sibling)
    copy.start()
    copy.wait()
    mtwo[...] = mown[...] + mcore[...]
    copies = [
        remote(mtwo, mx.at[s - 1], m_ssem.at[s], m_rsem.at[s], peer(0, s)) for s in (1, 2, 3)
    ]
    for c in copies:
        c.start()
    for c in copies:
        c.wait()
    mfour[...] = mtwo[...] + mx[0] + mx[1] + mx[2]
    mz[pl.ds(z, 1)] = mfour[...].reshape(1, 8, 128)
    for s in (1, 2, 3):
        remote(mfour, mz.at[z], m_ssem.at[3 + s], m_rsem.at[3 + s], peer(1, s)).start()
    for s in (1, 2, 3):
        remote(mfour, mz.at[(z + 4 - s) % 4], m_ssem.at[3 + s], m_rsem.at[3 + s], peer(1, s)).wait()
    my[pl.ds(y, 1)] = mz[...].reshape(1, 4, 8, 128)
    for s in (1, 2, 3):
        remote(mz, my.at[y], m_ssem.at[6 + s], m_rsem.at[6 + s], peer(2, s)).start()
    for s in (1, 2, 3):
        remote(mz, my.at[(y + 4 - s) % 4], m_ssem.at[6 + s], m_rsem.at[6 + s], peer(2, s)).wait()
    masks = my[...].reshape(128, 128).astype(BF16)

    own = owner[...]
    at = slot[...]
    e = (own & 3) * 32 + ((own >> 3) & 3) * 8 + ((own >> 5) & 3) * 2 + ((own >> 2) & 1)
    lanes = lax.broadcasted_iota(jnp.int32, (SLOTS, 128), 1)
    by_owner = jnp.where(e == lanes, 1.0, 0.0).astype(BF16)
    keeps = jnp.dot(by_owner, masks, preferred_element_type=F32)
    keep = jnp.sum(jnp.where(at == lanes, keeps, 0.0), axis=1, keepdims=True)
    keep = jnp.where((at & 15) == 0, 1.0, keep)
    code = jnp.where(keep > 0.5, (e * 128 + at).astype(F32), -1.0)

    sub = lax.broadcasted_iota(jnp.int32, (SLOTS, SLOTS), 0)
    lan = lax.broadcasted_iota(jnp.int32, (SLOTS, SLOTS), 1)
    eye = sub == lan
    sub_f = sub.astype(F32)

    def to_row(col):
        return jnp.sum(jnp.where(eye, col, 0.0), axis=0, keepdims=True)

    def axis_shift(m, axis):
        digit = (m.astype(jnp.int32) >> (8, 10, 12)[axis]) & 3
        return ((digit + 4 - here[axis]) & 3).astype(F32)

    def route(col, axis):
        line = to_row(col)
        twin = jnp.max(jnp.where((col == line) & (sub < lan), 1.0, 0.0), axis=0, keepdims=True)
        first = (line >= 0.0) & (twin < 0.5)
        shift_col, shift_line = axis_shift(col, axis), axis_shift(line, axis)
        ahead = first & (shift_line == shift_col) & (line < col)
        rank = jnp.sum(jnp.where(ahead, 1.0, 0.0), axis=1, keepdims=True)
        place = jnp.where((col >= 0.0) & (rank < CAP), shift_col * CAP + rank, -1.0)
        over = jnp.max(jnp.where((col >= 0.0) & (rank >= CAP), 1.0, 0.0), axis=0, keepdims=True)
        goes = sub_f == to_row(place)
        passed = jnp.max(jnp.where(goes, line, -1.0), axis=1, keepdims=True)
        return jnp.where(goes, 1.0, 0.0).astype(BF16), passed, over

    def send_header(phase, p, passed):
        hsend[phase, p] = jnp.broadcast_to(passed, (SLOTS, 128))
        for s in (1, 2, 3):
            remote(
                hsend.at[phase, p, pl.ds(s * CAP, CAP)],
                hrecv.at[phase, p, pl.ds((s - 1) * CAP, CAP)],
                h_ssem.at[phase, p],
                h_rsem.at[phase, p],
                peer(AXES[p][phase], s),
            ).start()

    def take_header(phase, p):
        remote(
            hsend.at[phase, p, pl.ds(CAP, 3 * CAP)],
            hrecv.at[phase, p],
            h_ssem.at[phase, p],
            h_rsem.at[phase, p],
            peer(AXES[p][phase], 1),
        ).wait()
        return jnp.concatenate([hsend[phase, p, 0:CAP, 0:1], hrecv[phase, p, :, 0:1]], axis=0)

    overs = []
    for p in range(3):
        table, passed, over = route(code, AXES[p][0])
        tabs[0, p] = table
        overs.append(over)
        send_header(0, p, passed)

    def later_tables(phase):
        for p in range(3):
            table, passed, over = route(take_header(phase - 1, p), AXES[p][phase])
            tabs[phase, p] = table
            overs.append(over)
            send_header(phase, p, passed)

    def last_tables():
        for p in range(3):
            col = take_header(2, p)
            whole = col.astype(jnp.int32)
            block = (whole & 127) + jnp.where(((whole >> 7) & 1) == core, 96, 0)
            block = jnp.where(col >= 0.0, block.astype(F32), -1.0)
            tabs[3, p] = jnp.where(sub_f == to_row(block), 1.0, 0.0).astype(BF16)

    def split_dot(table, values):
        high = values.astype(BF16)
        low = (values - high.astype(F32)).astype(BF16)
        return jnp.dot(table, high, preferred_element_type=F32) + jnp.dot(
            table, low, preferred_element_type=F32
        )

    recvs = (None, recv1, recv2, recv3)

    def rows_of(phase, i):
        if phase == 0:
            return buf[i]
        return jnp.concatenate([buf[i, 0:CAP, :], recvs[phase][i]], axis=0)

    def chunk_wait(phase, n, r0, rows):
        if phase == 0:
            pltpu.make_async_copy(
                buf.at[pl.ds(r0, rows)], buf.at[pl.ds(r0, rows)], child_sem.at[n]
            ).wait()
        else:
            ref = recvs[phase].at[pl.ds(r0, rows)]
            remote(ref, ref, send_sem.at[phase - 1, n], recv_sem.at[phase - 1, n], sibling).wait_recv()

    def forward(phase, n):
        _, p, r0, rows = CHUNKS[n]
        chunk_wait(phase, n, r0, rows)
        table = tabs[phase, p]

        def body(it, carry):
            for h in range(2):
                i = r0 + it * 4 + h * 2
                both = jnp.concatenate([rows_of(phase, i), rows_of(phase, i + 1)], axis=1)
                got = split_dot(table, both)
                for k in range(2):
                    part = got[:, k * 128:(k + 1) * 128]
                    if phase == 0:
                        buf[i + k] = part
                    else:
                        buf[i + k, 0:CAP, :] = part[0:CAP]
                        recvs[phase][i + k] = part[CAP:]
            return carry

        lax.fori_loop(0, rows // 4, body, 0)
        for s in (1, 2, 3):
            if phase == 0:
                src = buf.at[pl.ds(r0, rows), pl.ds(s * CAP, CAP), :]
            else:
                src = recvs[phase].at[pl.ds(r0, rows), pl.ds((s - 1) * CAP, CAP), :]
            remote(
                src,
                recvs[phase + 1].at[pl.ds(r0, rows), pl.ds((s - 1) * CAP, CAP), :],
                send_sem.at[phase, n],
                recv_sem.at[phase, n],
                peer(AXES[p][phase], s),
            ).start()

    def finish(n):
        _, p, r0, rows = CHUNKS[n]
        chunk_wait(3, n, r0, rows)
        table = tabs[3, p]

        def body(it, carry):
            for h in range(2):
                i = r0 + it * 4 + h * 2
                both = jnp.concatenate([rows_of(3, i), rows_of(3, i + 1)], axis=1)
                got = split_dot(table, both)
                for k in range(2):
                    part = got[:, k * 128:(k + 1) * 128]
                    recv3[i + k, 0:96, :] = part[0:96]
                    for a in range(6):
                        fbuf[a, i + k] = fbuf[a, i + k] + part[96 + a * 16:112 + a * 16]
            return carry

        lax.fori_loop(0, rows // 4, body, 0)
        remote(
            recv3.at[pl.ds(r0, rows), pl.ds(0, 96), :],
            sib.at[pl.ds(r0, rows)],
            sib_ssem.at[n],
            sib_rsem.at[n],
            sibling,
        ).start()

    def from_sibling(n):
        _, p, r0, rows = CHUNKS[n]
        ref = sib.at[pl.ds(r0, rows)]
        remote(ref, ref, sib_ssem.at[n], sib_rsem.at[n], sibling).wait_recv()

        def body(it, carry):
            i = r0 + it
            got = sib[i]
            for a in range(6):
                fbuf[a, i] = fbuf[a, i] + got[a * 16:a * 16 + 16]
            return carry

        lax.fori_loop(0, rows, body, 0)
        pltpu.make_async_copy(
            fbuf.at[:, pl.ds(r0, rows)], out.at[:, pl.ds(r0, rows)], out_sem.at[n]
        ).start()

    for n in range(N_CHUNKS):
        forward(0, n)
    later_tables(1)
    for n in range(N_CHUNKS):
        forward(1, n)
        if n == 2:
            later_tables(2)
    for n in range(N_CHUNKS):
        forward(2, n)
        if n == 2:
            last_tables()
            total = overs[0]
            for o in overs[1:]:
                total = jnp.maximum(total, o)
            fsend[0] = jnp.broadcast_to(total, (8, 128))
        if n in (3, 5, 7):
            step = (n - 3) // 2
            for s in (1, 2, 3):
                remote(fsend.at[step], frecv.at[step, s - 1], f_ssem.at[step, s - 1],
                       f_rsem.at[step, s - 1], peer(step, s)).start()
        if n in (4, 6, 8):
            step = (n - 4) // 2
            for s in (1, 2, 3):
                remote(fsend.at[step], frecv.at[step, s - 1], f_ssem.at[step, s - 1],
                       f_rsem.at[step, s - 1], peer(step, s)).wait()
            fsend[step + 1] = fsend[step] + frecv[step, 0] + frecv[step, 1] + frecv[step, 2]
    remote(fsend.at[3], frecv.at[3, 0], f_ssem.at[3, 0], f_rsem.at[3, 0], sibling).start()
    front_in.wait()
    for n in range(N_CHUNKS):
        finish(n)
        if n >= 1:
            from_sibling(n - 1)
    from_sibling(N_CHUNKS - 1)
    remote(fsend.at[3], frecv.at[3, 0], f_ssem.at[3, 0], f_rsem.at[3, 0], sibling).wait()
    flag[...] = fsend[3] + frecv[3, 0]
    for n, (_, _, r0, rows) in enumerate(CHUNKS):
        for phase in range(3):
            ref = recvs[phase + 1].at[pl.ds(r0, rows)]
            remote(ref, ref, send_sem.at[phase, n], recv_sem.at[phase, n], sibling).wait_send()
        ref = sib.at[pl.ds(r0, rows)]
        remote(ref, ref, sib_ssem.at[n], sib_rsem.at[n], sibling).wait_send()
        pltpu.make_async_copy(
            fbuf.at[:, pl.ds(r0, rows)], out.at[:, pl.ds(r0, rows)], out_sem.at[n]
        ).wait()


def exchange(child, front, owner, slot, mask_row):
    dma = pltpu.SemaphoreType.DMA
    vmem = pl.BlockSpec(memory_space=pltpu.VMEM)
    hbm = pl.BlockSpec(memory_space=pl.ANY)
    return pl.pallas_call(
        exchange_kernel,
        out_shape=(
            jax.ShapeDtypeStruct((6, 128, 16, 128), F32),
            jax.ShapeDtypeStruct((8, 128), F32),
        ),
        in_specs=[hbm, hbm, vmem, vmem, vmem],
        out_specs=(hbm, vmem),
        scratch_shapes=[
            pltpu.VMEM((128, SLOTS, 128), F32),
            pltpu.VMEM((128, 3 * CAP, 128), F32),
            pltpu.VMEM((128, 3 * CAP, 128), F32),
            pltpu.VMEM((128, 3 * CAP, 128), F32),
            pltpu.VMEM((128, 96, 128), F32),
            pltpu.VMEM((6, 128, 16, 128), F32),
            pltpu.VMEM((4, 3, SLOTS, SLOTS), BF16),
            pltpu.VMEM((8, 128), F32),
            pltpu.VMEM((8, 128), F32),
            pltpu.VMEM((8, 128), F32),
            pltpu.VMEM((3, 8, 128), F32),
            pltpu.VMEM((8, 128), F32),
            pltpu.VMEM((4, 8, 128), F32),
            pltpu.VMEM((4, 4, 8, 128), F32),
            pltpu.VMEM((3, 3, SLOTS, 128), F32),
            pltpu.VMEM((3, 3, 3 * CAP, 128), F32),
            pltpu.VMEM((4, 8, 128), F32),
            pltpu.VMEM((4, 3, 8, 128), F32),
            dma((N_CHUNKS,)),
            dma,
            dma((N_CHUNKS,)),
            dma((3, N_CHUNKS)),
            dma((3, N_CHUNKS)),
            dma((N_CHUNKS,)),
            dma((N_CHUNKS,)),
            dma((10,)),
            dma((10,)),
            dma((3, 3)),
            dma((3, 3)),
            dma((4, 3)),
            dma((4, 3)),
        ],
        compiler_params=pltpu.CompilerParams(
            collective_id=0, has_side_effects=True, vmem_limit_bytes=62 * 2**20
        ),
        name="tile_exchange",
    )(child, front, owner, slot, mask_row)


def any_exchange(front, child_tiles, owner_map, parent_slot):
    devices = lax.axis_size("row") * lax.axis_size("col")
    slots_total = 96
    tile_area = child_tiles.shape[1]
    owner_dev = owner_map[:, 0]
    owner_hits = (owner_dev[:, None] == jnp.arange(devices, dtype=jnp.int32)[None, :]).astype(
        jnp.int32
    )
    earlier = jnp.cumsum(owner_hits, axis=0) - owner_hits
    tile_rank = jnp.sum(earlier * owner_hits, axis=1)
    send_slot = owner_dev * MOST + tile_rank
    outgoing = jnp.zeros((devices * MOST, tile_area), F32).at[send_slot].set(child_tiles)
    targets = jnp.full((devices * MOST,), slots_total, jnp.int32).at[send_slot].set(parent_slot)
    arrived = lax.all_to_all(
        outgoing.reshape(devices, MOST, tile_area), ("row", "col"), 0, 0, tiled=True
    ).reshape(devices * MOST, tile_area)
    places = lax.all_to_all(
        targets.reshape(devices, MOST), ("row", "col"), 0, 0, tiled=True
    ).reshape(devices * MOST)
    blocks = jnp.zeros((slots_total, tile_area), F32).at[places].add(arrived, mode="drop")
    return front + blocks.reshape(6, 16, 128, 128).transpose(0, 2, 1, 3)


def per_device(front, mask, child_tiles, owner_map, parent_slot, pivot_order, inv_pivot):
    n_row = lax.axis_size("row")
    n_col = lax.axis_size("col")
    blk_rows, block_size, blk_cols = 6, 128, 16
    rows_here = blk_rows * block_size
    panel_size = 512
    panel_local = 1
    front4 = front.reshape(6, 128, 16, 128)
    child4 = child_tiles.reshape(24, 8, 128, 128).transpose(0, 2, 1, 3)
    mask_row = jnp.pad(mask.reshape(1, 96).astype(F32), ((0, 7), (0, 32)))
    quick, flag = exchange(child4, front4, owner_map, parent_slot.reshape(192, 1), mask_row)
    assembled = lax.cond(
        flag[0, 0] > 0.5,
        lambda: any_exchange(front4, child_tiles, owner_map, parent_slot),
        lambda: quick,
    )
    assembled = assembled.reshape(rows_here, blk_cols * block_size)
    own_panel = assembled[:, : panel_local * block_size]
    gathered = lax.all_gather(own_panel, "col", axis=1, tiled=True)
    panel_cols = (
        gathered.reshape(rows_here, n_col, panel_local, block_size)
        .transpose(0, 2, 1, 3)
        .reshape(rows_here, panel_size)
    )
    permuted = jnp.take(panel_cols, pivot_order, axis=1)
    factor = jnp.dot(permuted, inv_pivot, precision=lax.Precision.HIGHEST)
    col_here = lax.axis_index("col")
    window_local = blk_cols * n_col // n_row
    window_mine = permuted[: window_local * block_size]
    everything = lax.all_gather(window_mine, "row", axis=0, tiled=True).reshape(
        n_row, window_local, block_size, panel_size
    )
    block_index = jnp.arange(blk_cols, dtype=jnp.int32) * n_col + col_here
    needed = everything[block_index % n_row, block_index // n_row]
    needed = needed.reshape(blk_cols * block_size, panel_size)
    trailing = needed[panel_local * block_size :]
    update = jnp.einsum("rp,cp->rc", factor, trailing, precision=lax.Precision.HIGHEST)
    keep_block = mask.reshape(blk_rows, blk_cols)[:, panel_local:] > 0
    schur_part = (assembled[:, panel_local * block_size :] - update).reshape(
        blk_rows, block_size, blk_cols - panel_local, block_size
    )
    schur_part = jnp.where(keep_block[:, None, :, None], schur_part, 0.0)
    factor_mine = lax.dynamic_slice_in_dim(
        factor.reshape(rows_here, panel_local, n_col, block_size), col_here, 1, 2
    ).reshape(rows_here, panel_local * block_size)
    result = jnp.concatenate(
        [factor_mine, schur_part.reshape(rows_here, (blk_cols - panel_local) * block_size)], 1
    )
    return result.reshape(front.shape)


def solution(mesh):
    placed = (
        P(None, "row", None, None, "col", None),
        P(None, "row", None, "col"),
        P(("row", "col"), None),
        P(("row", "col"), None),
        P(("row", "col")),
        P(),
        P(),
    )
    return jax.shard_map(
        per_device,
        mesh=mesh,
        in_specs=placed,
        out_specs=P(None, "row", None, None, "col", None),
        check_vma=False,
    )
```

```python
import functools

import jax
import jax.numpy as jnp
from jax import lax
from jax.experimental import pallas as pl
from jax.experimental.pallas import tpu as pltpu
from jax.sharding import PartitionSpec as P

MOST = 2
CAP = 48
SLOTS = 4 * CAP
MESH = pl.DeviceIdType.MESH
F32 = jnp.float32
BF16 = jnp.bfloat16
GROUPS = ((8, 8, 8), (16, 12, 12), (12, 12, 16), (8, 8, 8))
N_GROUPS = len(GROUPS)
CHUNKS = []
SPANS = []
_row = 0
for _k, _sizes in enumerate(GROUPS):
    SPANS.append((_row, sum(_sizes)))
    for _p, _n in enumerate(_sizes):
        CHUNKS.append((_k, _p, _row, _n))
        _row += _n
N_CHUNKS = len(CHUNKS)
AXES = ((0, 1, 2), (1, 2, 0), (2, 0, 1))


def exchange_kernel(
    child, front, owner, slot, mask_row, out, panel, trail, flag,
    buf, recv1, recv2, recv3, sib, fbuf, pan, tabs, mown, mcore, mtwo, mx, mfour, mz, my,
    hsend, hrecv, fsend, frecv,
    child_sem, front_sem, out_sem, send_sem, recv_sem, sib_ssem, sib_rsem,
    m_ssem, m_rsem, h_ssem, h_rsem, f_ssem, f_rsem,
    pan_sem, y_ssem, y_rsem, a_ssem, a_rsem, b_ssem, b_rsem, c_ssem, c_rsem,
):
    row_at, y = lax.axis_index("row"), lax.axis_index("col")
    x, z, core = row_at // 8, (row_at // 2) % 4, row_at % 2

    def peer(axis, shift):
        if axis == 0:
            return (((x + shift) % 4) * 8 + z * 2 + core, y)
        if axis == 1:
            return (x * 8 + ((z + shift) % 4) * 2 + core, y)
        return (row_at, (y + shift) % 4)

    sibling = (row_at + 1 - 2 * core, y)
    here = (x, z, y)

    def remote(src, dst, ssem, rsem, to):
        return pltpu.make_async_remote_copy(
            src_ref=src, dst_ref=dst, send_sem=ssem, recv_sem=rsem, device_id=to, device_id_type=MESH
        )

    front_in = pltpu.make_async_copy(front, fbuf, front_sem)
    for n, (_, _, r0, rows) in enumerate(CHUNKS):

        def load(g, carry, n=n, r0=r0, rows=rows):
            pltpu.make_async_copy(
                child.at[g, pl.ds(r0, rows)],
                buf.at[pl.ds(r0, rows), pl.ds(pl.multiple_of(g * 8, 8), 8), :],
                child_sem.at[n],
            ).start()
            return carry

        lax.fori_loop(0, SLOTS // 8, load, 0)
    front_in.start()

    barrier = pltpu.get_barrier_semaphore()
    for axis in range(3):
        for shift in (1, 2, 3):
            pl.semaphore_signal(barrier, inc=1, device_id=peer(axis, shift), device_id_type=MESH)
    pl.semaphore_signal(barrier, inc=1, device_id=sibling, device_id_type=MESH)
    pl.semaphore_wait(barrier, 10)

    sub8 = lax.broadcasted_iota(jnp.int32, (8, 128), 0)
    mown[...] = jnp.where(sub8 == x * 2 + core, jnp.broadcast_to(mask_row[0:1, :], (8, 128)), 0.0)
    copy = remote(mown, mcore, m_ssem.at[0], m_rsem.at[0], sibling)
    copy.start()
    copy.wait()
    mtwo[...] = mown[...] + mcore[...]
    copies = [
        remote(mtwo, mx.at[s - 1], m_ssem.at[s], m_rsem.at[s], peer(0, s)) for s in (1, 2, 3)
    ]
    for c in copies:
        c.start()
    for c in copies:
        c.wait()
    mfour[...] = mtwo[...] + mx[0] + mx[1] + mx[2]
    mz[pl.ds(z, 1)] = mfour[...].reshape(1, 8, 128)
    for s in (1, 2, 3):
        remote(mfour, mz.at[z], m_ssem.at[3 + s], m_rsem.at[3 + s], peer(1, s)).start()
    for s in (1, 2, 3):
        remote(mfour, mz.at[(z + 4 - s) % 4], m_ssem.at[3 + s], m_rsem.at[3 + s], peer(1, s)).wait()
    my[pl.ds(y, 1)] = mz[...].reshape(1, 4, 8, 128)
    for s in (1, 2, 3):
        remote(mz, my.at[y], m_ssem.at[6 + s], m_rsem.at[6 + s], peer(2, s)).start()
    for s in (1, 2, 3):
        remote(mz, my.at[(y + 4 - s) % 4], m_ssem.at[6 + s], m_rsem.at[6 + s], peer(2, s)).wait()
    masks = my[...].reshape(128, 128).astype(BF16)

    own = owner[...]
    at = slot[...]
    e = (own & 3) * 32 + ((own >> 3) & 3) * 8 + ((own >> 5) & 3) * 2 + ((own >> 2) & 1)
    lanes = lax.broadcasted_iota(jnp.int32, (SLOTS, 128), 1)
    by_owner = jnp.where(e == lanes, 1.0, 0.0).astype(BF16)
    keeps = jnp.dot(by_owner, masks, preferred_element_type=F32)
    keep = jnp.sum(jnp.where(at == lanes, keeps, 0.0), axis=1, keepdims=True)
    keep = jnp.where((at & 15) == 0, 1.0, keep)
    code = jnp.where(keep > 0.5, (e * 128 + at).astype(F32), -1.0)

    sub = lax.broadcasted_iota(jnp.int32, (SLOTS, SLOTS), 0)
    lan = lax.broadcasted_iota(jnp.int32, (SLOTS, SLOTS), 1)
    eye = sub == lan
    sub_f = sub.astype(F32)

    def to_row(col):
        return jnp.sum(jnp.where(eye, col, 0.0), axis=0, keepdims=True)

    def axis_shift(m, axis):
        digit = (m.astype(jnp.int32) >> (8, 10, 12)[axis]) & 3
        return ((digit + 4 - here[axis]) & 3).astype(F32)

    def route(col, axis):
        line = to_row(col)
        twin = jnp.max(jnp.where((col == line) & (sub < lan), 1.0, 0.0), axis=0, keepdims=True)
        first = (line >= 0.0) & (twin < 0.5)
        shift_col, shift_line = axis_shift(col, axis), axis_shift(line, axis)
        ahead = first & (shift_line == shift_col) & (line < col)
        rank = jnp.sum(jnp.where(ahead, 1.0, 0.0), axis=1, keepdims=True)
        place = jnp.where((col >= 0.0) & (rank < CAP), shift_col * CAP + rank, -1.0)
        over = jnp.max(jnp.where((col >= 0.0) & (rank >= CAP), 1.0, 0.0), axis=0, keepdims=True)
        goes = sub_f == to_row(place)
        passed = jnp.max(jnp.where(goes, line, -1.0), axis=1, keepdims=True)
        return jnp.where(goes, 1.0, 0.0).astype(BF16), passed, over

    def send_header(phase, p, passed):
        hsend[phase, p] = jnp.broadcast_to(passed, (SLOTS, 128))
        for s in (1, 2, 3):
            remote(
                hsend.at[phase, p, pl.ds(s * CAP, CAP)],
                hrecv.at[phase, p, pl.ds((s - 1) * CAP, CAP)],
                h_ssem.at[phase, p],
                h_rsem.at[phase, p],
                peer(AXES[p][phase], s),
            ).start()

    def take_header(phase, p):
        remote(
            hsend.at[phase, p, pl.ds(CAP, 3 * CAP)],
            hrecv.at[phase, p],
            h_ssem.at[phase, p],
            h_rsem.at[phase, p],
            peer(AXES[p][phase], 1),
        ).wait()
        return jnp.concatenate([hsend[phase, p, 0:CAP, 0:1], hrecv[phase, p, :, 0:1]], axis=0)

    overs = []
    for p in range(3):
        table, passed, over = route(code, AXES[p][0])
        tabs[0, p] = table
        overs.append(over)
        send_header(0, p, passed)

    def later_tables(phase):
        for p in range(3):
            table, passed, over = route(take_header(phase - 1, p), AXES[p][phase])
            tabs[phase, p] = table
            overs.append(over)
            send_header(phase, p, passed)

    def last_tables():
        for p in range(3):
            col = take_header(2, p)
            whole = col.astype(jnp.int32)
            block = (whole & 127) + jnp.where(((whole >> 7) & 1) == core, 96, 0)
            block = jnp.where(col >= 0.0, block.astype(F32), -1.0)
            tabs[3, p] = jnp.where(sub_f == to_row(block), 1.0, 0.0).astype(BF16)

    def split_dot(table, values):
        high = values.astype(BF16)
        low = (values - high.astype(F32)).astype(BF16)
        return jnp.dot(table, high, preferred_element_type=F32) + jnp.dot(
            table, low, preferred_element_type=F32
        )

    recvs = (None, recv1, recv2, recv3)

    def rows_of(phase, i):
        if phase == 0:
            return buf[i]
        return jnp.concatenate([buf[i, 0:CAP, :], recvs[phase][i]], axis=0)

    def chunk_wait(phase, n, r0, rows):
        if phase == 0:
            pltpu.make_async_copy(
                buf.at[pl.ds(r0, rows)], buf.at[pl.ds(r0, rows)], child_sem.at[n]
            ).wait()
        else:
            ref = recvs[phase].at[pl.ds(r0, rows)]
            remote(ref, ref, send_sem.at[phase - 1, n], recv_sem.at[phase - 1, n], sibling).wait_recv()

    def forward(phase, n):
        _, p, r0, rows = CHUNKS[n]
        chunk_wait(phase, n, r0, rows)
        table = tabs[phase, p]

        def body(it, carry):
            for h in range(2):
                i = r0 + it * 4 + h * 2
                both = jnp.concatenate([rows_of(phase, i), rows_of(phase, i + 1)], axis=1)
                got = split_dot(table, both)
                for k in range(2):
                    part = got[:, k * 128:(k + 1) * 128]
                    if phase == 0:
                        buf[i + k] = part
                    else:
                        buf[i + k, 0:CAP, :] = part[0:CAP]
                        recvs[phase][i + k] = part[CAP:]
            return carry

        lax.fori_loop(0, rows // 4, body, 0)
        for s in (1, 2, 3):
            if phase == 0:
                src = buf.at[pl.ds(r0, rows), pl.ds(s * CAP, CAP), :]
            else:
                src = recvs[phase].at[pl.ds(r0, rows), pl.ds((s - 1) * CAP, CAP), :]
            remote(
                src,
                recvs[phase + 1].at[pl.ds(r0, rows), pl.ds((s - 1) * CAP, CAP), :],
                send_sem.at[phase, n],
                recv_sem.at[phase, n],
                peer(AXES[p][phase], s),
            ).start()

    def finish(n):
        _, p, r0, rows = CHUNKS[n]
        chunk_wait(3, n, r0, rows)
        table = tabs[3, p]

        def body(it, carry):
            for h in range(2):
                i = r0 + it * 4 + h * 2
                both = jnp.concatenate([rows_of(3, i), rows_of(3, i + 1)], axis=1)
                got = split_dot(table, both)
                for k in range(2):
                    part = got[:, k * 128:(k + 1) * 128]
                    recv3[i + k, 0:96, :] = part[0:96]
                    for a in range(6):
                        fbuf[a, i + k] = fbuf[a, i + k] + part[96 + a * 16:112 + a * 16]
            return carry

        lax.fori_loop(0, rows // 4, body, 0)
        remote(
            recv3.at[pl.ds(r0, rows), pl.ds(0, 96), :],
            sib.at[pl.ds(r0, rows)],
            sib_ssem.at[n],
            sib_rsem.at[n],
            sibling,
        ).start()

    def from_sibling(n):
        _, p, r0, rows = CHUNKS[n]
        ref = sib.at[pl.ds(r0, rows)]
        remote(ref, ref, sib_ssem.at[n], sib_rsem.at[n], sibling).wait_recv()

        def body(it, carry):
            i = r0 + it
            got = sib[i]
            for a in range(6):
                fbuf[a, i] = fbuf[a, i] + got[a * 16:a * 16 + 16]
            return carry

        lax.fori_loop(0, rows, body, 0)
        pltpu.make_async_copy(
            fbuf.at[:, pl.ds(r0, rows)], out.at[:, pl.ds(r0, rows)], out_sem.at[n]
        ).start()

    holds = core == y % 2
    on_line = z % 2 == y // 2
    mine = 2 * x + z // 2
    other = 2 * x + ((z + 2) % 4) // 2
    lower = 2 * x
    source = jnp.logical_and(holds, on_line)
    off_line = jnp.logical_and(holds, jnp.logical_not(on_line))

    def pan_copy(g):
        r0, rows = SPANS[g]
        return pltpu.make_async_copy(
            pan.at[:, pl.ds(r0, rows)], panel.at[y, :, pl.ds(r0, rows)], pan_sem.at[g]
        )

    def y_copy(g, s, at):
        r0, rows = SPANS[g]
        return remote(
            pan.at[:, pl.ds(r0, rows)], panel.at[at, :, pl.ds(r0, rows)],
            y_ssem.at[g, s - 1], y_rsem.at[g, s - 1], peer(2, s),
        )

    def panel_out(g):
        r0, rows = SPANS[g]

        def body(it, carry):
            i = pl.multiple_of(r0 + it * 4, 4)
            for a in range(6):
                for k in range(4):
                    pan[a, pl.ds(i + k, 1), :] = fbuf[a, i + k, 0:1, :]
            return carry

        lax.fori_loop(0, rows // 4, body, 0)
        pan_copy(g).start()
        for s in (1, 2, 3):
            y_copy(g, s, y).start()

    def trail_at(g, place, half):
        r0, rows = SPANS[g]
        return trail.at[place, :, half, pl.ds(r0, rows)]

    def source_copy(g, half, sems, s, place):
        r0, rows = SPANS[g]
        return remote(
            panel.at[:, half, pl.ds(r0, rows)], trail_at(g, place, half),
            sems[0].at[g, 0, s - 1], sems[1].at[g, 0, s - 1], peer(half, s),
        )

    def own_copy(g, half):
        r0, rows = SPANS[g]
        return pltpu.make_async_copy(
            panel.at[:, half, pl.ds(r0, rows)], trail_at(g, mine, half), pan_sem.at[N_GROUPS + half * N_GROUPS + g]
        )

    a_sems, b_sems = (a_ssem, a_rsem), (b_ssem, b_rsem)

    def from_x(s):
        return 2 * ((x + 4 - s) % 4)

    def panel_rows(g):
        pan_copy(g).wait()
        for s in (1, 2, 3):
            y_copy(g, s, (y + 4 - s) % 4).wait_recv()

        @pl.when(source)
        def _():
            for half in (0, 1):
                own_copy(g, half).start()
                for s in (1, 2, 3):
                    source_copy(g, half, (a_sems, b_sems)[half], s, mine).start()

    def a_line(g, s, i, base):
        place = 2 * i + base // 2
        ref = trail_at(g, place, 0)
        return remote(ref, ref, a_ssem.at[g, 1 + i, s - 1], a_rsem.at[g, 1 + i, s - 1], peer(1, s))

    def b_line(g, s, zz, at):
        ref = trail_at(g, 2 * at + zz, 1)
        return remote(ref, ref, b_ssem.at[g, 1 + zz, s - 1], b_rsem.at[g, 1 + zz, s - 1], peer(0, s))

    def panel_lines(g):
        @pl.when(source)
        def _():
            for half in (0, 1):
                own_copy(g, half).wait()
            for s in (1, 2, 3):
                source_copy(g, 0, a_sems, s, from_x(s) + z // 2).wait_recv()
            for i in range(4):
                for s in (1, 3, 2):
                    a_line(g, s, i, z).start()
            source_copy(g, 1, b_sems, 2, other).wait_recv()

        @pl.when(off_line)
        def _():
            for s in (1, 3):
                source_copy(g, 1, b_sems, s, lower + ((z + 4 - s) % 4) // 2).wait_recv()

        @pl.when(holds)
        def _():
            for zz in (0, 1):
                for s in (1, 2, 3):
                    b_line(g, s, zz, x).start()

    def to_sibling(g):
        r0, rows = SPANS[g]
        ref = trail.at[:, :, :, pl.ds(r0, rows)]
        return remote(ref, ref, c_ssem.at[g], c_rsem.at[g], sibling)

    def panel_cores(g):
        @pl.when(source)
        def _():
            for i in range(4):
                a_line(g, 2, i, (z + 2) % 4).wait_recv()

        @pl.when(off_line)
        def _():
            for i in range(4):
                for s in (1, 3):
                    a_line(g, s, i, (z + 4 - s) % 4).wait_recv()

        @pl.when(holds)
        def _():
            for zz in (0, 1):
                for s in (1, 2, 3):
                    b_line(g, s, zz, (x + 4 - s) % 4).wait_recv()
            to_sibling(g).start()

    def panel_end(g):
        for s in (1, 2, 3):
            y_copy(g, s, y).wait_send()

        @pl.when(source)
        def _():
            for half in (0, 1):
                for s in (1, 2, 3):
                    source_copy(g, half, (a_sems, b_sems)[half], s, mine).wait_send()
            for i in range(4):
                for s in (1, 2, 3):
                    a_line(g, s, i, z).wait_send()

        @pl.when(holds)
        def _():
            for zz in (0, 1):
                for s in (1, 2, 3):
                    b_line(g, s, zz, x).wait_send()
            to_sibling(g).wait_send()

        @pl.when(jnp.logical_not(holds))
        def _():
            to_sibling(g).wait_recv()

    def flag_copies(step):
        return [
            remote(fsend.at[step], frecv.at[step, s - 1], f_ssem.at[step, s - 1],
                   f_rsem.at[step, s - 1], peer(step, s))
            for s in (1, 2, 3)
        ]

    flag_last = remote(fsend.at[3], frecv.at[3, 0], f_ssem.at[3, 0], f_rsem.at[3, 0], sibling)

    def flag_step(step):
        if step > 0:
            for c in flag_copies(step - 1):
                c.wait()
            fsend[step] = (
                fsend[step - 1] + frecv[step - 1, 0] + frecv[step - 1, 1] + frecv[step - 1, 2]
            )
        for c in flag_copies(step) if step < 3 else [flag_last]:
            c.start()

    flags_done = 0
    steps = sorted((stage + g, stage, g) for stage in range(8) for g in range(N_GROUPS))
    for _, stage, g in steps:
        chunks = [n for n in range(N_CHUNKS) if CHUNKS[n][0] == g]
        if stage < 3:
            if g == 0 and stage > 0:
                later_tables(stage)
            for n in chunks:
                forward(stage, n)
        elif stage == 3:
            if g == 0:
                last_tables()
                total = overs[0]
                for o in overs[1:]:
                    total = jnp.maximum(total, o)
                fsend[0] = jnp.broadcast_to(total, (8, 128))
                front_in.wait()
            for n in chunks:
                finish(n)
        elif stage == 4:
            for n in chunks:
                from_sibling(n)
            panel_out(g)
        elif stage == 5:
            panel_rows(g)
        elif stage == 6:
            panel_lines(g)
        else:
            panel_cores(g)
        if stage >= 3 and flags_done < 4:
            flag_step(flags_done)
            flags_done += 1
    flag_last.wait()
    flag[...] = fsend[3] + frecv[3, 0]
    for n, (_, _, r0, rows) in enumerate(CHUNKS):
        for phase in range(3):
            ref = recvs[phase + 1].at[pl.ds(r0, rows)]
            remote(ref, ref, send_sem.at[phase, n], recv_sem.at[phase, n], sibling).wait_send()
        ref = sib.at[pl.ds(r0, rows)]
        remote(ref, ref, sib_ssem.at[n], sib_rsem.at[n], sibling).wait_send()
        pltpu.make_async_copy(
            fbuf.at[:, pl.ds(r0, rows)], out.at[:, pl.ds(r0, rows)], out_sem.at[n]
        ).wait()
    for g in range(N_GROUPS):
        panel_end(g)


def exchange(child, front, owner, slot, mask_row):
    dma = pltpu.SemaphoreType.DMA
    vmem = pl.BlockSpec(memory_space=pltpu.VMEM)
    hbm = pl.BlockSpec(memory_space=pl.ANY)
    return pl.pallas_call(
        exchange_kernel,
        out_shape=(
            jax.ShapeDtypeStruct((6, 128, 16, 128), F32),
            jax.ShapeDtypeStruct((4, 6, 128, 128), F32),
            jax.ShapeDtypeStruct((8, 4, 2, 128, 128), F32),
            jax.ShapeDtypeStruct((8, 128), F32),
        ),
        in_specs=[hbm, hbm, vmem, vmem, vmem],
        out_specs=(hbm, hbm, hbm, vmem),
        scratch_shapes=[
            pltpu.VMEM((128, SLOTS, 128), F32),
            pltpu.VMEM((128, 3 * CAP, 128), F32),
            pltpu.VMEM((128, 3 * CAP, 128), F32),
            pltpu.VMEM((128, 3 * CAP, 128), F32),
            pltpu.VMEM((128, 96, 128), F32),
            pltpu.VMEM((6, 128, 16, 128), F32),
            pltpu.VMEM((6, 128, 128), F32),
            pltpu.VMEM((4, 3, SLOTS, SLOTS), BF16),
            pltpu.VMEM((8, 128), F32),
            pltpu.VMEM((8, 128), F32),
            pltpu.VMEM((8, 128), F32),
            pltpu.VMEM((3, 8, 128), F32),
            pltpu.VMEM((8, 128), F32),
            pltpu.VMEM((4, 8, 128), F32),
            pltpu.VMEM((4, 4, 8, 128), F32),
            pltpu.VMEM((3, 3, SLOTS, 128), F32),
            pltpu.VMEM((3, 3, 3 * CAP, 128), F32),
            pltpu.VMEM((4, 8, 128), F32),
            pltpu.VMEM((4, 3, 8, 128), F32),
            dma((N_CHUNKS,)),
            dma,
            dma((N_CHUNKS,)),
            dma((3, N_CHUNKS)),
            dma((3, N_CHUNKS)),
            dma((N_CHUNKS,)),
            dma((N_CHUNKS,)),
            dma((10,)),
            dma((10,)),
            dma((3, 3)),
            dma((3, 3)),
            dma((4, 3)),
            dma((4, 3)),
            dma((3 * N_GROUPS,)),
            dma((N_GROUPS, 3)),
            dma((N_GROUPS, 3)),
            dma((N_GROUPS, 5, 3)),
            dma((N_GROUPS, 5, 3)),
            dma((N_GROUPS, 3, 3)),
            dma((N_GROUPS, 3, 3)),
            dma((N_GROUPS,)),
            dma((N_GROUPS,)),
        ],
        compiler_params=pltpu.CompilerParams(
            collective_id=0, has_side_effects=True, vmem_limit_bytes=62 * 2**20
        ),
        name="tile_exchange",
    )(child, front, owner, slot, mask_row)


def schur_kernel(
    col_at, mask, order, inverse, panel, trail, front, out,
    n_high, n_low, m_high, m_low, t_high, t_low,
):
    def split(values):
        high = values.astype(BF16)
        return high, (values - high.astype(F32)).astype(BF16)

    def dot(a, b):
        return jnp.dot(a, b, preferred_element_type=F32)

    def dot_t(a, b):
        return lax.dot_general(a, b, (((1,), (1,)), ((), ())), preferred_element_type=F32)

    def three(left, right, how):
        return how(left[0], right[0]) + how(left[0], right[1]) + how(left[1], right[0])

    @pl.when(pl.program_id(0) == 0)
    def _():
        sub = lax.broadcasted_iota(jnp.int32, (512, 512), 0)
        place = jnp.where(sub == order[...], 1.0, 0.0).astype(BF16)
        for part, n_ref, m_ref in zip(split(inverse[...]), (n_high, n_low), (m_high, m_low)):
            rows = dot(place, part).astype(BF16)
            n_ref[...] = rows
            m_ref[...] = dot_t(rows, place).astype(BF16)
        for half in range(2):
            for m in range(8):
                for k in range(4):
                    high, low = split(trail[m, k, half])
                    t_high[half * 8 + m, :, k * 128:(k + 1) * 128] = high
                    t_low[half * 8 + m, :, k * 128:(k + 1) * 128] = low

    pair = pl.program_id(0)
    rows = jnp.concatenate(
        [jnp.concatenate([panel[k, a] for k in range(4)], axis=1) for a in range(2)], axis=0
    )
    rows = split(rows)
    mine = pl.ds(pl.multiple_of(col_at[0] * 128, 128), 128)
    factor = three(rows, (n_high[:, mine], n_low[:, mine]), dot)
    turned = split(three(rows, (m_high[...], m_low[...]), dot))
    for a in range(2):
        out[pl.ds(a * 2048, 128, stride=16), :] = factor[a * 128:(a + 1) * 128]
    for first in range(0, 16, 2):
        cols = (
            t_high[first:first + 2].reshape(256, 512),
            t_low[first:first + 2].reshape(256, 512),
        )
        update = three(turned, cols, dot_t)
        for b in (first, first + 1):
            if b == 0:
                continue
            for a in range(2):
                at = pl.ds(a * 2048 + b, 128, stride=16)
                part = update[a * 128:(a + 1) * 128, (b - first) * 128:(b - first + 1) * 128]
                keep = mask[pair * 2 + a, b] > 0
                out[at, :] = jnp.where(keep, front[at, :] - part, 0.0)


def finish_front(col_at, mask, order, inverse, panel, trail, assembled):
    smem = pl.BlockSpec(memory_space=pltpu.SMEM)
    return pl.pallas_call(
        schur_kernel,
        grid=(3,),
        out_shape=jax.ShapeDtypeStruct((12288, 128), F32),
        in_specs=[
            smem,
            smem,
            pl.BlockSpec((1, 512), lambda i: (0, 0)),
            pl.BlockSpec((512, 512), lambda i: (0, 0)),
            pl.BlockSpec((4, 2, 128, 128), lambda i: (0, i, 0, 0)),
            pl.BlockSpec((8, 4, 2, 128, 128), lambda i: (0, 0, 0, 0, 0)),
            pl.BlockSpec((4096, 128), lambda i: (i, 0)),
        ],
        out_specs=pl.BlockSpec((4096, 128), lambda i: (i, 0)),
        scratch_shapes=[
            pltpu.VMEM((512, 512), BF16),
            pltpu.VMEM((512, 512), BF16),
            pltpu.VMEM((512, 512), BF16),
            pltpu.VMEM((512, 512), BF16),
            pltpu.VMEM((16, 128, 512), BF16),
            pltpu.VMEM((16, 128, 512), BF16),
        ],
        compiler_params=pltpu.CompilerParams(vmem_limit_bytes=40 * 2**20),
        name="schur",
    )(col_at, mask, order, inverse, panel, trail, assembled)


def any_front(front, mask, child_tiles, owner_map, parent_slot, pivot_order, inv_pivot):
    n_row = lax.axis_size("row")
    n_col = lax.axis_size("col")
    devices = n_row * n_col
    blk_rows = front.shape[0]
    block_size = front.shape[2]
    blk_cols = front.shape[3]
    rows_here = blk_rows * block_size
    local_width = blk_cols * block_size
    panel_size = inv_pivot.shape[0]
    panel_local = panel_size // (block_size * n_col)
    slots_total = blk_rows * blk_cols
    tile_area = child_tiles.shape[1]
    owner_dev = owner_map[:, 0]
    owner_hits = (owner_dev[:, None] == jnp.arange(devices, dtype=jnp.int32)[None, :]).astype(
        jnp.int32
    )
    earlier = jnp.cumsum(owner_hits, axis=0) - owner_hits
    tile_rank = jnp.sum(earlier * owner_hits, axis=1)
    send_slot = owner_dev * MOST + tile_rank
    outgoing = jnp.zeros((devices * MOST, tile_area), jnp.float32).at[send_slot].set(child_tiles)
    targets = jnp.full((devices * MOST,), slots_total, jnp.int32).at[send_slot].set(parent_slot)
    arrived, places = (
        lax.all_to_all(
            outgoing.reshape(devices, MOST, tile_area),
            ("row", "col"),
            split_axis=0,
            concat_axis=0,
            tiled=True,
        ),
        lax.all_to_all(
            targets.reshape(devices, MOST), ("row", "col"), split_axis=0, concat_axis=0, tiled=True
        ),
    )
    arrived = arrived.reshape(devices * MOST, tile_area)
    places = places.reshape(devices * MOST)
    blocks = jnp.zeros((slots_total, tile_area), jnp.float32).at[places].add(arrived, mode="drop")
    contrib = (
        blocks.reshape(blk_rows, blk_cols, block_size, block_size)
        .transpose(0, 2, 1, 3)
        .reshape(rows_here, local_width)
    )
    assembled = front.reshape(rows_here, local_width) + contrib
    own_panel = assembled[:, : panel_local * block_size]
    gathered = lax.all_gather(own_panel, "col", axis=1, tiled=True)
    panel_cols = (
        gathered.reshape(rows_here, n_col, panel_local, block_size)
        .transpose(0, 2, 1, 3)
        .reshape(rows_here, panel_size)
    )
    permuted = jnp.take(panel_cols, pivot_order, axis=1)
    factor = jnp.dot(permuted, inv_pivot, precision=lax.Precision.HIGHEST)
    col_here = lax.axis_index("col")
    window_local = blk_cols * n_col // n_row
    window_mine = permuted[: window_local * block_size]
    everything = lax.all_gather(window_mine, "row", axis=0, tiled=True).reshape(
        n_row, window_local, block_size, panel_size
    )
    block_index = jnp.arange(blk_cols, dtype=jnp.int32) * n_col + col_here
    needed = everything[block_index % n_row, block_index // n_row]
    needed = needed.reshape(blk_cols * block_size, panel_size)
    trailing = needed[panel_local * block_size :]
    update = jnp.einsum("rp,cp->rc", factor, trailing, precision=lax.Precision.HIGHEST)
    keep_block = mask.reshape(blk_rows, blk_cols)[:, panel_local:] > 0
    schur_part = (assembled[:, panel_local * block_size :] - update).reshape(
        blk_rows, block_size, blk_cols - panel_local, block_size
    )
    schur_part = jnp.where(keep_block[:, None, :, None], schur_part, 0.0)
    factor_mine = lax.dynamic_slice_in_dim(
        factor.reshape(rows_here, panel_local, n_col, block_size), col_here, 1, 2
    ).reshape(rows_here, panel_local * block_size)
    result = jnp.concatenate(
        [factor_mine, schur_part.reshape(rows_here, (blk_cols - panel_local) * block_size)], 1
    )
    return result.reshape(front.shape)


def per_device(front, mask, child_tiles, owner_map, parent_slot, pivot_order, inv_pivot):
    child4 = child_tiles.reshape(24, 8, 128, 128).transpose(0, 2, 1, 3)
    mask_here = mask.reshape(6, 16)
    mask_row = jnp.pad(mask.reshape(1, 96).astype(F32), ((0, 7), (0, 32)))
    assembled, panel, trail, flag = exchange(
        child4,
        front.reshape(6, 128, 16, 128),
        owner_map.reshape(192, 1),
        parent_slot.reshape(192, 1),
        mask_row,
    )
    col_at = lax.axis_index("col").astype(jnp.int32).reshape(1)
    return lax.cond(
        flag[0, 0] > 0.5,
        lambda: any_front(
            front, mask, child_tiles, owner_map, parent_slot, pivot_order, inv_pivot
        ),
        lambda: finish_front(
            col_at,
            mask_here,
            pivot_order.reshape(1, 512),
            inv_pivot,
            panel,
            trail,
            assembled.reshape(12288, 128),
        ).reshape(front.shape),
    )


def solution(mesh):
    placed = (
        P(None, "row", None, None, "col", None),
        P(None, "row", None, "col"),
        P(("row", "col"), None),
        P(("row", "col"), None),
        P(("row", "col")),
        P(),
        P(),
    )
    return jax.shard_map(
        per_device,
        mesh=mesh,
        in_specs=placed,
        out_specs=P(None, "row", None, None, "col", None),
        check_vma=False,
    )
```

```python
import functools

import jax
import jax.numpy as jnp
from jax import lax
from jax.experimental import pallas as pl
from jax.experimental.pallas import tpu as pltpu
from jax.sharding import PartitionSpec as P

MOST = 2
CAP = 48
SLOTS = 4 * CAP
MESH = pl.DeviceIdType.MESH
F32 = jnp.float32
BF16 = jnp.bfloat16
GROUPS = ((6, 4, 6), (4, 6, 6), (8, 8, 8), (8, 8, 8), (6, 4, 6), (4, 6, 6), (6, 6, 4))
N_GROUPS = len(GROUPS)
CHUNKS = []
SPANS = []
_row = 0
for _k, _sizes in enumerate(GROUPS):
    SPANS.append((_row, sum(_sizes)))
    for _p, _n in enumerate(_sizes):
        CHUNKS.append((_k, _p, _row, _n))
        _row += _n
N_CHUNKS = len(CHUNKS)
AXES = ((0, 1, 2), (1, 2, 0), (2, 0, 1))


def exchange_kernel(
    child, front, owner, slot, mask, out, panel, trail, flag,
    buf, recv1, recv2, recv3, sib, fbuf, pan, tabs, mown, mx, mfour, my,
    hsend, hrecv, fsend, frecv,
    child_sem, front_sem, out_sem, send_sem, recv_sem, sib_ssem, sib_rsem,
    m_ssem, m_rsem, h_ssem, h_rsem, f_ssem, f_rsem,
    pan_sem, y_ssem, y_rsem, a_ssem, a_rsem, b_ssem, b_rsem, c_ssem, c_rsem,
):
    row_at, y = lax.axis_index("row"), lax.axis_index("col")
    x, z, core = row_at // 8, (row_at // 2) % 4, row_at % 2

    def peer(axis, shift):
        if axis == 0:
            return (((x + shift) % 4) * 8 + z * 2 + core, y)
        if axis == 1:
            return (x * 8 + ((z + shift) % 4) * 2 + core, y)
        return (row_at, (y + shift) % 4)

    sibling = (row_at + 1 - 2 * core, y)
    here = (x, z, y)

    def remote(src, dst, ssem, rsem, to):
        return pltpu.make_async_remote_copy(
            src_ref=src, dst_ref=dst, send_sem=ssem, recv_sem=rsem, device_id=to, device_id_type=MESH
        )

    front_in = pltpu.make_async_copy(front, fbuf, front_sem)

    def load_group(g):
        r0, rows = SPANS[g]

        def load(i, carry):
            pltpu.make_async_copy(
                child.at[i, pl.ds(r0, rows)],
                buf.at[pl.ds(r0, rows), pl.ds(pl.multiple_of(i * 8, 8), 8), :],
                child_sem.at[g],
            ).start()
            return carry

        lax.fori_loop(0, SLOTS // 8, load, 0)

    line_to = [
        (i, (((x + i // 2) % 4) * 8 + z * 2 + (core + i) % 2, y)) for i in range(1, 8)
    ]
    plane_to = [
        (i, (x * 8 + ((z + i // 4) % 4) * 2 + core, (y + i) % 4)) for i in range(1, 16)
    ]
    barrier = pltpu.get_barrier_semaphore()
    for _, to in line_to + plane_to:
        pl.semaphore_signal(barrier, inc=1, device_id=to, device_id_type=MESH)

    sub16 = lax.broadcasted_iota(jnp.int32, (16, 128), 0)
    lan16 = lax.broadcasted_iota(jnp.int32, (16, 128), 1)
    line = jnp.zeros((8, 128), F32)
    for a in range(6):
        here_a = jnp.broadcast_to(mask[a].astype(F32), (8, 16)).astype(BF16)
        spread = jnp.where(lan16 == sub16 + a * 16, 1.0, 0.0).astype(BF16)
        line = line + jnp.dot(here_a, spread, preferred_element_type=F32)
    sub8 = lax.broadcasted_iota(jnp.int32, (8, 128), 0)
    mown[...] = jnp.where(sub8 == x * 2 + core, line, 0.0)
    load_group(0)
    pl.semaphore_wait(barrier, 22)
    copies = [remote(mown, mx.at[i - 1], m_ssem.at[i], m_rsem.at[i], to) for i, to in line_to]
    for c in copies:
        c.start()
    load_group(1)
    for c in copies:
        c.wait()
    gathered = mown[...]
    for i in range(7):
        gathered = gathered + mx[i]
    mfour[...] = gathered
    my[pl.ds(y, 1), pl.ds(z, 1)] = gathered.reshape(1, 1, 8, 128)
    for i, to in plane_to:
        remote(mfour, my.at[y, z], m_ssem.at[7 + i], m_rsem.at[7 + i], to).start()
    for g in range(2, N_GROUPS):
        load_group(g)
    front_in.start()
    for i, to in plane_to:
        at = my.at[(y + 16 - i) % 4, (z + 4 - i // 4) % 4]
        remote(mfour, at, m_ssem.at[7 + i], m_rsem.at[7 + i], to).wait()
    masks = my[...].reshape(128, 128).astype(BF16)

    sub = lax.broadcasted_iota(jnp.int32, (SLOTS, SLOTS), 0)
    lan = lax.broadcasted_iota(jnp.int32, (SLOTS, SLOTS), 1)
    eye = sub == lan
    sub_f = sub.astype(F32)

    def to_col(line):
        values = jnp.where(eye, line.astype(F32), 0.0)
        return jnp.sum(values, axis=1, keepdims=True).astype(jnp.int32)

    own = to_col(owner[...])
    at = to_col(slot[...])
    e = (own & 3) * 32 + ((own >> 3) & 3) * 8 + ((own >> 5) & 3) * 2 + ((own >> 2) & 1)
    lanes = lax.broadcasted_iota(jnp.int32, (SLOTS, 128), 1)
    by_owner = jnp.where(e == lanes, 1.0, 0.0).astype(BF16)
    keeps = jnp.dot(by_owner, masks, preferred_element_type=F32)
    keep = jnp.sum(jnp.where(at == lanes, keeps, 0.0), axis=1, keepdims=True)
    keep = jnp.where((at & 15) == 0, 1.0, keep)
    code = jnp.where(keep > 0.5, (e * 128 + at).astype(F32), -1.0)

    def to_row(col):
        return jnp.sum(jnp.where(eye, col, 0.0), axis=0, keepdims=True)

    def axis_shift(m, axis):
        digit = (m.astype(jnp.int32) >> (8, 10, 12)[axis]) & 3
        return ((digit + 4 - here[axis]) & 3).astype(F32)

    def route(col, axis):
        line = to_row(col)
        twin = jnp.max(jnp.where((col == line) & (sub < lan), 1.0, 0.0), axis=0, keepdims=True)
        first = (line >= 0.0) & (twin < 0.5)
        shift_col, shift_line = axis_shift(col, axis), axis_shift(line, axis)
        ahead = first & (shift_line == shift_col) & (line < col)
        rank = jnp.sum(jnp.where(ahead, 1.0, 0.0), axis=1, keepdims=True)
        place = jnp.where((col >= 0.0) & (rank < CAP), shift_col * CAP + rank, -1.0)
        over = jnp.max(jnp.where((col >= 0.0) & (rank >= CAP), 1.0, 0.0), axis=0, keepdims=True)
        goes = sub_f == to_row(place)
        passed = jnp.max(jnp.where(goes, line, -1.0), axis=1, keepdims=True)
        return jnp.where(goes, 1.0, 0.0).astype(BF16), passed, over

    def send_header(phase, p, passed):
        hsend[phase, p] = jnp.broadcast_to(passed, (SLOTS, 128))
        for s in (1, 2, 3):
            remote(
                hsend.at[phase, p, pl.ds(s * CAP, CAP)],
                hrecv.at[phase, p, pl.ds((s - 1) * CAP, CAP)],
                h_ssem.at[phase, p],
                h_rsem.at[phase, p],
                peer(AXES[p][phase], s),
            ).start()

    def take_header(phase, p):
        remote(
            hsend.at[phase, p, pl.ds(CAP, 3 * CAP)],
            hrecv.at[phase, p],
            h_ssem.at[phase, p],
            h_rsem.at[phase, p],
            peer(AXES[p][phase], 1),
        ).wait()
        return jnp.concatenate([hsend[phase, p, 0:CAP, 0:1], hrecv[phase, p, :, 0:1]], axis=0)

    overs = []

    def first_table(p):
        table, passed, over = route(code, AXES[p][0])
        tabs[0, p] = table
        overs.append(over)
        send_header(0, p, passed)

    def later_tables(phase):
        for p in range(3):
            table, passed, over = route(take_header(phase - 1, p), AXES[p][phase])
            tabs[phase, p] = table
            overs.append(over)
            send_header(phase, p, passed)

    def last_tables():
        for p in range(3):
            col = take_header(2, p)
            whole = col.astype(jnp.int32)
            block = (whole & 127) + jnp.where(((whole >> 7) & 1) == core, 96, 0)
            block = jnp.where(col >= 0.0, block.astype(F32), -1.0)
            tabs[3, p] = jnp.where(sub_f == to_row(block), 1.0, 0.0).astype(BF16)

    def split_dot(table, values):
        high = values.astype(BF16)
        low = (values - high.astype(F32)).astype(BF16)
        return jnp.dot(table, high, preferred_element_type=F32) + jnp.dot(
            table, low, preferred_element_type=F32
        )

    recvs = (None, recv1, recv2, recv3)

    def rows_of(phase, i):
        if phase == 0:
            return buf[i]
        return jnp.concatenate([buf[i, 0:CAP, :], recvs[phase][i]], axis=0)

    def chunk_wait(phase, n, r0, rows):
        if phase == 0:
            g, p = CHUNKS[n][:2]
            if p == 0:
                ref = buf.at[pl.ds(SPANS[g][0], SPANS[g][1])]
                pltpu.make_async_copy(ref, ref, child_sem.at[g]).wait()
        else:
            ref = recvs[phase].at[pl.ds(r0, rows)]
            remote(ref, ref, send_sem.at[phase - 1, n], recv_sem.at[phase - 1, n], sibling).wait_recv()

    def forward(phase, n):
        _, p, r0, rows = CHUNKS[n]
        chunk_wait(phase, n, r0, rows)
        table = tabs[phase, p]

        def body(it, carry):
            i = r0 + it * 2
            both = jnp.concatenate([rows_of(phase, i), rows_of(phase, i + 1)], axis=1)
            got = split_dot(table, both)
            for k in range(2):
                part = got[:, k * 128:(k + 1) * 128]
                if phase == 0:
                    buf[i + k] = part
                else:
                    buf[i + k, 0:CAP, :] = part[0:CAP]
                    recvs[phase][i + k] = part[CAP:]
            return carry

        lax.fori_loop(0, rows // 2, body, 0)
        for s in (1, 2, 3):
            if phase == 0:
                src = buf.at[pl.ds(r0, rows), pl.ds(s * CAP, CAP), :]
            else:
                src = recvs[phase].at[pl.ds(r0, rows), pl.ds((s - 1) * CAP, CAP), :]
            remote(
                src,
                recvs[phase + 1].at[pl.ds(r0, rows), pl.ds((s - 1) * CAP, CAP), :],
                send_sem.at[phase, n],
                recv_sem.at[phase, n],
                peer(AXES[p][phase], s),
            ).start()

    def finish(n):
        _, p, r0, rows = CHUNKS[n]
        chunk_wait(3, n, r0, rows)
        table = tabs[3, p]

        def body(it, carry):
            i = r0 + it * 2
            both = jnp.concatenate([rows_of(3, i), rows_of(3, i + 1)], axis=1)
            got = split_dot(table, both)
            for k in range(2):
                part = got[:, k * 128:(k + 1) * 128]
                recv3[i + k, 0:96, :] = part[0:96]
                for a in range(6):
                    fbuf[a, i + k] = fbuf[a, i + k] + part[96 + a * 16:112 + a * 16]
            return carry

        lax.fori_loop(0, rows // 2, body, 0)
        remote(
            recv3.at[pl.ds(r0, rows), pl.ds(0, 96), :],
            sib.at[pl.ds(r0, rows)],
            sib_ssem.at[n],
            sib_rsem.at[n],
            sibling,
        ).start()

    def from_sibling(n):
        _, p, r0, rows = CHUNKS[n]
        ref = sib.at[pl.ds(r0, rows)]
        remote(ref, ref, sib_ssem.at[n], sib_rsem.at[n], sibling).wait_recv()

        def body(it, carry):
            i = r0 + it
            got = sib[i]
            for a in range(6):
                fbuf[a, i] = fbuf[a, i] + got[a * 16:a * 16 + 16]
            return carry

        lax.fori_loop(0, rows, body, 0)
        pltpu.make_async_copy(
            fbuf.at[:, pl.ds(r0, rows)], out.at[:, pl.ds(r0, rows)], out_sem.at[n]
        ).start()

    holds = core == y % 2
    on_line = z % 2 == y // 2
    mine = 2 * x + z // 2
    other = 2 * x + ((z + 2) % 4) // 2
    lower = 2 * x
    source = jnp.logical_and(holds, on_line)
    off_line = jnp.logical_and(holds, jnp.logical_not(on_line))

    def pan_copy(g):
        r0, rows = SPANS[g]
        return pltpu.make_async_copy(
            pan.at[:, pl.ds(r0, rows)], panel.at[y, :, pl.ds(r0, rows)], pan_sem.at[g]
        )

    def y_copy(g, s, at):
        r0, rows = SPANS[g]
        return remote(
            pan.at[:, pl.ds(r0, rows)], panel.at[at, :, pl.ds(r0, rows)],
            y_ssem.at[g, s - 1], y_rsem.at[g, s - 1], peer(2, s),
        )

    def panel_out(g):
        r0, rows = SPANS[g]

        def body(it, carry):
            i = pl.multiple_of(r0 + it * 4, 4)
            for a in range(6):
                for k in range(4):
                    pan[a, pl.ds(i + k, 1), :] = fbuf[a, i + k, 0:1, :]
            return carry

        lax.fori_loop(0, rows // 4, body, 0)
        pan_copy(g).start()
        for s in (1, 2, 3):
            y_copy(g, s, y).start()

    def trail_at(g, place, half):
        r0, rows = SPANS[g]
        return trail.at[place, :, half, pl.ds(r0, rows)]

    def source_copy(g, half, sems, s, place):
        r0, rows = SPANS[g]
        return remote(
            panel.at[:, half, pl.ds(r0, rows)], trail_at(g, place, half),
            sems[0].at[g, 0, s - 1], sems[1].at[g, 0, s - 1], peer(half, s),
        )

    def own_copy(g, half):
        r0, rows = SPANS[g]
        return pltpu.make_async_copy(
            panel.at[:, half, pl.ds(r0, rows)], trail_at(g, mine, half), pan_sem.at[N_GROUPS + half * N_GROUPS + g]
        )

    a_sems, b_sems = (a_ssem, a_rsem), (b_ssem, b_rsem)

    def from_x(s):
        return 2 * ((x + 4 - s) % 4)

    def panel_rows(g):
        pan_copy(g).wait()
        for s in (1, 2, 3):
            y_copy(g, s, (y + 4 - s) % 4).wait_recv()

        @pl.when(source)
        def _():
            for half in (0, 1):
                own_copy(g, half).start()
                for s in (1, 2, 3):
                    source_copy(g, half, (a_sems, b_sems)[half], s, mine).start()

    def a_line(g, s, i, base):
        place = 2 * i + base // 2
        ref = trail_at(g, place, 0)
        return remote(ref, ref, a_ssem.at[g, 1 + i, s - 1], a_rsem.at[g, 1 + i, s - 1], peer(1, s))

    def b_line(g, s, zz, at):
        ref = trail_at(g, 2 * at + zz, 1)
        return remote(ref, ref, b_ssem.at[g, 1 + zz, s - 1], b_rsem.at[g, 1 + zz, s - 1], peer(0, s))

    def panel_lines(g):
        @pl.when(source)
        def _():
            for half in (0, 1):
                own_copy(g, half).wait()
            for s in (1, 2, 3):
                source_copy(g, 0, a_sems, s, from_x(s) + z // 2).wait_recv()
            for i in range(4):
                for s in (1, 3, 2):
                    a_line(g, s, i, z).start()
            source_copy(g, 1, b_sems, 2, other).wait_recv()

        @pl.when(off_line)
        def _():
            for s in (1, 3):
                source_copy(g, 1, b_sems, s, lower + ((z + 4 - s) % 4) // 2).wait_recv()

        @pl.when(holds)
        def _():
            for zz in (0, 1):
                for s in (1, 2, 3):
                    b_line(g, s, zz, x).start()

    def to_sibling(g):
        r0, rows = SPANS[g]
        ref = trail.at[:, :, :, pl.ds(r0, rows)]
        return remote(ref, ref, c_ssem.at[g], c_rsem.at[g], sibling)

    def panel_cores(g):
        @pl.when(source)
        def _():
            for i in range(4):
                a_line(g, 2, i, (z + 2) % 4).wait_recv()

        @pl.when(off_line)
        def _():
            for i in range(4):
                for s in (1, 3):
                    a_line(g, s, i, (z + 4 - s) % 4).wait_recv()

        @pl.when(holds)
        def _():
            for zz in (0, 1):
                for s in (1, 2, 3):
                    b_line(g, s, zz, (x + 4 - s) % 4).wait_recv()
            to_sibling(g).start()

    def panel_end(g):
        for s in (1, 2, 3):
            y_copy(g, s, y).wait_send()

        @pl.when(source)
        def _():
            for half in (0, 1):
                for s in (1, 2, 3):
                    source_copy(g, half, (a_sems, b_sems)[half], s, mine).wait_send()
            for i in range(4):
                for s in (1, 2, 3):
                    a_line(g, s, i, z).wait_send()

        @pl.when(holds)
        def _():
            for zz in (0, 1):
                for s in (1, 2, 3):
                    b_line(g, s, zz, x).wait_send()
            to_sibling(g).wait_send()

        @pl.when(jnp.logical_not(holds))
        def _():
            to_sibling(g).wait_recv()

    def flag_copies(step):
        return [
            remote(fsend.at[step], frecv.at[step, s - 1], f_ssem.at[step, s - 1],
                   f_rsem.at[step, s - 1], peer(step, s))
            for s in (1, 2, 3)
        ]

    flag_last = remote(fsend.at[3], frecv.at[3, 0], f_ssem.at[3, 0], f_rsem.at[3, 0], sibling)

    def flag_step(step):
        if step > 0:
            for c in flag_copies(step - 1):
                c.wait()
            fsend[step] = (
                fsend[step - 1] + frecv[step - 1, 0] + frecv[step - 1, 1] + frecv[step - 1, 2]
            )
        for c in flag_copies(step) if step < 3 else [flag_last]:
            c.start()

    flags_done = 0
    steps = sorted((stage + g, stage, g) for stage in range(8) for g in range(N_GROUPS))
    for _, stage, g in steps:
        chunks = [n for n in range(N_CHUNKS) if CHUNKS[n][0] == g]
        if stage < 3:
            if g == 0 and stage > 0:
                later_tables(stage)
            for n in chunks:
                if stage == 0 and g == 0:
                    first_table(CHUNKS[n][1])
                forward(stage, n)
        elif stage == 3:
            if g == 0:
                last_tables()
                total = overs[0]
                for o in overs[1:]:
                    total = jnp.maximum(total, o)
                fsend[0] = jnp.broadcast_to(total, (8, 128))
                front_in.wait()
            for n in chunks:
                finish(n)
        elif stage == 4:
            for n in chunks:
                from_sibling(n)
            panel_out(g)
        elif stage == 5:
            panel_rows(g)
        elif stage == 6:
            panel_lines(g)
        else:
            panel_cores(g)
        if stage >= 3 and flags_done < 4:
            flag_step(flags_done)
            flags_done += 1
    flag_last.wait()
    flag[0, 0] = jnp.max(fsend[3] + frecv[3, 0]).astype(jnp.int32)
    for n, (_, _, r0, rows) in enumerate(CHUNKS):
        for phase in range(3):
            ref = recvs[phase + 1].at[pl.ds(r0, rows)]
            remote(ref, ref, send_sem.at[phase, n], recv_sem.at[phase, n], sibling).wait_send()
        ref = sib.at[pl.ds(r0, rows)]
        remote(ref, ref, sib_ssem.at[n], sib_rsem.at[n], sibling).wait_send()
        pltpu.make_async_copy(
            fbuf.at[:, pl.ds(r0, rows)], out.at[:, pl.ds(r0, rows)], out_sem.at[n]
        ).wait()
    for g in range(N_GROUPS):
        panel_end(g)


def exchange(child, front, owner, slot, mask):
    dma = pltpu.SemaphoreType.DMA
    vmem = pl.BlockSpec(memory_space=pltpu.VMEM)
    hbm = pl.BlockSpec(memory_space=pl.ANY)
    return pl.pallas_call(
        exchange_kernel,
        out_shape=(
            jax.ShapeDtypeStruct((6, 128, 16, 128), F32),
            jax.ShapeDtypeStruct((4, 6, 128, 128), F32),
            jax.ShapeDtypeStruct((8, 4, 2, 128, 128), F32),
            jax.ShapeDtypeStruct((1, 1), jnp.int32),
        ),
        in_specs=[hbm, hbm, vmem, vmem, vmem],
        out_specs=(hbm, hbm, hbm, pl.BlockSpec(memory_space=pltpu.SMEM)),
        scratch_shapes=[
            pltpu.VMEM((128, SLOTS, 128), F32),
            pltpu.VMEM((128, 3 * CAP, 128), F32),
            pltpu.VMEM((128, 3 * CAP, 128), F32),
            pltpu.VMEM((128, 3 * CAP, 128), F32),
            pltpu.VMEM((128, 96, 128), F32),
            pltpu.VMEM((6, 128, 16, 128), F32),
            pltpu.VMEM((6, 128, 128), F32),
            pltpu.VMEM((4, 3, SLOTS, SLOTS), BF16),
            pltpu.VMEM((8, 128), F32),
            pltpu.VMEM((7, 8, 128), F32),
            pltpu.VMEM((8, 128), F32),
            pltpu.VMEM((4, 4, 8, 128), F32),
            pltpu.VMEM((3, 3, SLOTS, 128), F32),
            pltpu.VMEM((3, 3, 3 * CAP, 128), F32),
            pltpu.VMEM((4, 8, 128), F32),
            pltpu.VMEM((4, 3, 8, 128), F32),
            dma((N_GROUPS,)),
            dma,
            dma((N_CHUNKS,)),
            dma((3, N_CHUNKS)),
            dma((3, N_CHUNKS)),
            dma((N_CHUNKS,)),
            dma((N_CHUNKS,)),
            dma((23,)),
            dma((23,)),
            dma((3, 3)),
            dma((3, 3)),
            dma((4, 3)),
            dma((4, 3)),
            dma((3 * N_GROUPS,)),
            dma((N_GROUPS, 3)),
            dma((N_GROUPS, 3)),
            dma((N_GROUPS, 5, 3)),
            dma((N_GROUPS, 5, 3)),
            dma((N_GROUPS, 3, 3)),
            dma((N_GROUPS, 3, 3)),
            dma((N_GROUPS,)),
            dma((N_GROUPS,)),
        ],
        compiler_params=pltpu.CompilerParams(
            collective_id=0, has_side_effects=True, vmem_limit_bytes=62 * 2**20
        ),
        name="tile_exchange",
    )(child, front, owner, slot, mask)


def schur_kernel(
    col_at, mask, order, inverse, panel, trail, front, out,
    n_high, n_low, m_high, m_low, t_high, t_low,
):
    def split(values):
        high = values.astype(BF16)
        return high, (values - high.astype(F32)).astype(BF16)

    def dot(a, b):
        return jnp.dot(a, b, preferred_element_type=F32)

    def dot_t(a, b):
        return lax.dot_general(a, b, (((1,), (1,)), ((), ())), preferred_element_type=F32)

    def three(left, right, how):
        return how(left[0], right[0]) + how(left[0], right[1]) + how(left[1], right[0])

    @pl.when(pl.program_id(0) == 0)
    def _():
        sub = lax.broadcasted_iota(jnp.int32, (512, 512), 0)
        place = jnp.where(sub == order[...], 1.0, 0.0).astype(BF16)
        for part, n_ref, m_ref in zip(split(inverse[...]), (n_high, n_low), (m_high, m_low)):
            rows = dot(place, part).astype(BF16)
            n_ref[...] = rows
            m_ref[...] = dot_t(rows, place).astype(BF16)
        for half in range(2):
            for m in range(8):
                for k in range(4):
                    high, low = split(trail[m, k, half])
                    t_high[half * 8 + m, :, k * 128:(k + 1) * 128] = high
                    t_low[half * 8 + m, :, k * 128:(k + 1) * 128] = low

    pair = pl.program_id(0)
    rows = jnp.concatenate(
        [jnp.concatenate([panel[k, a] for k in range(4)], axis=1) for a in range(2)], axis=0
    )
    rows = split(rows)
    mine = pl.ds(pl.multiple_of(col_at[0] * 128, 128), 128)
    factor = three(rows, (n_high[:, mine], n_low[:, mine]), dot)
    turned = split(three(rows, (m_high[...], m_low[...]), dot))
    for a in range(2):
        out[pl.ds(a * 2048, 128, stride=16), :] = factor[a * 128:(a + 1) * 128]
    for first in range(0, 16, 2):
        cols = (
            t_high[first:first + 2].reshape(256, 512),
            t_low[first:first + 2].reshape(256, 512),
        )
        update = three(turned, cols, dot_t)
        for b in (first, first + 1):
            if b == 0:
                continue
            for a in range(2):
                at = pl.ds(a * 2048 + b, 128, stride=16)
                part = update[a * 128:(a + 1) * 128, (b - first) * 128:(b - first + 1) * 128]
                keep = mask[pair * 2 + a, b] > 0
                out[at, :] = jnp.where(keep, front[at, :] - part, 0.0)


def finish_front(col_at, mask, order, inverse, panel, trail, assembled):
    smem = pl.BlockSpec(memory_space=pltpu.SMEM)
    return pl.pallas_call(
        schur_kernel,
        grid=(3,),
        out_shape=jax.ShapeDtypeStruct((12288, 128), F32),
        in_specs=[
            smem,
            smem,
            pl.BlockSpec((1, 512), lambda i: (0, 0)),
            pl.BlockSpec((512, 512), lambda i: (0, 0)),
            pl.BlockSpec((4, 2, 128, 128), lambda i: (0, i, 0, 0)),
            pl.BlockSpec((8, 4, 2, 128, 128), lambda i: (0, 0, 0, 0, 0)),
            pl.BlockSpec((4096, 128), lambda i: (i, 0)),
        ],
        out_specs=pl.BlockSpec((4096, 128), lambda i: (i, 0)),
        scratch_shapes=[
            pltpu.VMEM((512, 512), BF16),
            pltpu.VMEM((512, 512), BF16),
            pltpu.VMEM((512, 512), BF16),
            pltpu.VMEM((512, 512), BF16),
            pltpu.VMEM((16, 128, 512), BF16),
            pltpu.VMEM((16, 128, 512), BF16),
        ],
        compiler_params=pltpu.CompilerParams(vmem_limit_bytes=40 * 2**20),
        name="schur",
    )(col_at, mask, order, inverse, panel, trail, assembled)


def any_front(front, mask, child_tiles, owner_map, parent_slot, pivot_order, inv_pivot):
    n_row = lax.axis_size("row")
    n_col = lax.axis_size("col")
    devices = n_row * n_col
    blk_rows = front.shape[0]
    block_size = front.shape[2]
    blk_cols = front.shape[3]
    rows_here = blk_rows * block_size
    local_width = blk_cols * block_size
    panel_size = inv_pivot.shape[0]
    panel_local = panel_size // (block_size * n_col)
    slots_total = blk_rows * blk_cols
    tile_area = child_tiles.shape[1]
    owner_dev = owner_map[:, 0]
    owner_hits = (owner_dev[:, None] == jnp.arange(devices, dtype=jnp.int32)[None, :]).astype(
        jnp.int32
    )
    earlier = jnp.cumsum(owner_hits, axis=0) - owner_hits
    tile_rank = jnp.sum(earlier * owner_hits, axis=1)
    send_slot = owner_dev * MOST + tile_rank
    outgoing = jnp.zeros((devices * MOST, tile_area), jnp.float32).at[send_slot].set(child_tiles)
    targets = jnp.full((devices * MOST,), slots_total, jnp.int32).at[send_slot].set(parent_slot)
    arrived, places = (
        lax.all_to_all(
            outgoing.reshape(devices, MOST, tile_area),
            ("row", "col"),
            split_axis=0,
            concat_axis=0,
            tiled=True,
        ),
        lax.all_to_all(
            targets.reshape(devices, MOST), ("row", "col"), split_axis=0, concat_axis=0, tiled=True
        ),
    )
    arrived = arrived.reshape(devices * MOST, tile_area)
    places = places.reshape(devices * MOST)
    blocks = jnp.zeros((slots_total, tile_area), jnp.float32).at[places].add(arrived, mode="drop")
    contrib = (
        blocks.reshape(blk_rows, blk_cols, block_size, block_size)
        .transpose(0, 2, 1, 3)
        .reshape(rows_here, local_width)
    )
    assembled = front.reshape(rows_here, local_width) + contrib
    own_panel = assembled[:, : panel_local * block_size]
    gathered = lax.all_gather(own_panel, "col", axis=1, tiled=True)
    panel_cols = (
        gathered.reshape(rows_here, n_col, panel_local, block_size)
        .transpose(0, 2, 1, 3)
        .reshape(rows_here, panel_size)
    )
    permuted = jnp.take(panel_cols, pivot_order, axis=1)
    factor = jnp.dot(permuted, inv_pivot, precision=lax.Precision.HIGHEST)
    col_here = lax.axis_index("col")
    window_local = blk_cols * n_col // n_row
    window_mine = permuted[: window_local * block_size]
    everything = lax.all_gather(window_mine, "row", axis=0, tiled=True).reshape(
        n_row, window_local, block_size, panel_size
    )
    block_index = jnp.arange(blk_cols, dtype=jnp.int32) * n_col + col_here
    needed = everything[block_index % n_row, block_index // n_row]
    needed = needed.reshape(blk_cols * block_size, panel_size)
    trailing = needed[panel_local * block_size :]
    update = jnp.einsum("rp,cp->rc", factor, trailing, precision=lax.Precision.HIGHEST)
    keep_block = mask.reshape(blk_rows, blk_cols)[:, panel_local:] > 0
    schur_part = (assembled[:, panel_local * block_size :] - update).reshape(
        blk_rows, block_size, blk_cols - panel_local, block_size
    )
    schur_part = jnp.where(keep_block[:, None, :, None], schur_part, 0.0)
    factor_mine = lax.dynamic_slice_in_dim(
        factor.reshape(rows_here, panel_local, n_col, block_size), col_here, 1, 2
    ).reshape(rows_here, panel_local * block_size)
    result = jnp.concatenate(
        [factor_mine, schur_part.reshape(rows_here, (blk_cols - panel_local) * block_size)], 1
    )
    return result.reshape(front.shape)


def per_device(front, mask, child_tiles, owner_map, parent_slot, pivot_order, inv_pivot):
    child4 = child_tiles.reshape(24, 8, 128, 128).transpose(0, 2, 1, 3)
    mask_here = mask.reshape(6, 16)
    assembled, panel, trail, flag = exchange(
        child4,
        front.reshape(6, 128, 16, 128),
        owner_map.reshape(1, 192),
        parent_slot.reshape(1, 192),
        mask.reshape(6, 1, 16),
    )
    col_at = lax.axis_index("col").astype(jnp.int32).reshape(1)
    return lax.cond(
        flag[0, 0] > 0,
        lambda: any_front(
            front, mask, child_tiles, owner_map, parent_slot, pivot_order, inv_pivot
        ),
        lambda: finish_front(
            col_at,
            mask_here,
            pivot_order.reshape(1, 512),
            inv_pivot,
            panel,
            trail,
            assembled.reshape(12288, 128),
        ).reshape(front.shape),
    )


def solution(mesh):
    placed = (
        P(None, "row", None, None, "col", None),
        P(None, "row", None, "col"),
        P(("row", "col"), None),
        P(("row", "col"), None),
        P(("row", "col")),
        P(),
        P(),
    )
    return jax.shard_map(
        per_device,
        mesh=mesh,
        in_specs=placed,
        out_specs=P(None, "row", None, None, "col", None),
        check_vma=False,
    )
```

```python
import functools

import jax
import jax.numpy as jnp
from jax import lax
from jax.experimental import pallas as pl
from jax.experimental.pallas import tpu as pltpu
from jax.sharding import PartitionSpec as P

MOST = 2
CAP = 48
SLOTS = 4 * CAP
MESH = pl.DeviceIdType.MESH
F32 = jnp.float32
BF16 = jnp.bfloat16
GROUPS = ((6, 4, 6), (4, 6, 6), (8, 8, 8), (8, 8, 8), (6, 4, 6), (4, 6, 6), (6, 6, 4))
N_GROUPS = len(GROUPS)
CHUNKS = []
SPANS = []
_row = 0
for _k, _sizes in enumerate(GROUPS):
    SPANS.append((_row, sum(_sizes)))
    for _p, _n in enumerate(_sizes):
        CHUNKS.append((_k, _p, _row, _n))
        _row += _n
N_CHUNKS = len(CHUNKS)
AXES = ((0, 1, 2), (1, 2, 0), (2, 0, 1))


def exchange_kernel(
    child, front, owner, slot, mask, out, panel, trail, flag,
    buf, recv1, recv2, recv3, sib, fbuf, pan, tabs, mown, mx, mfour, my,
    hsend, hrecv, fsend, frecv,
    child_sem, front_sem, out_sem, send_sem, recv_sem, sib_ssem, sib_rsem,
    m_ssem, m_rsem, h_ssem, h_rsem, f_ssem, f_rsem,
    pan_sem, y_ssem, y_rsem, a_ssem, a_rsem, b_ssem, b_rsem, c_ssem, c_rsem,
):
    row_at, y = lax.axis_index("row"), lax.axis_index("col")
    x, z, core = row_at // 8, (row_at // 2) % 4, row_at % 2

    def peer(axis, shift):
        if axis == 0:
            return (((x + shift) % 4) * 8 + z * 2 + core, y)
        if axis == 1:
            return (x * 8 + ((z + shift) % 4) * 2 + core, y)
        return (row_at, (y + shift) % 4)

    sibling = (row_at + 1 - 2 * core, y)
    here = (x, z, y)

    def remote(src, dst, ssem, rsem, to):
        return pltpu.make_async_remote_copy(
            src_ref=src, dst_ref=dst, send_sem=ssem, recv_sem=rsem, device_id=to, device_id_type=MESH
        )

    front_in = pltpu.make_async_copy(front, fbuf, front_sem)

    def load_group(g):
        r0, rows = SPANS[g]

        def load(i, carry):
            pltpu.make_async_copy(
                child.at[i, pl.ds(r0, rows)],
                buf.at[pl.ds(r0, rows), pl.ds(pl.multiple_of(i * 8, 8), 8), :],
                child_sem.at[g],
            ).start()
            return carry

        lax.fori_loop(0, SLOTS // 8, load, 0)

    line_to = [
        (i, (((x + i // 2) % 4) * 8 + z * 2 + (core + i) % 2, y)) for i in range(1, 8)
    ]
    plane_to = [
        (i, (x * 8 + ((z + i // 4) % 4) * 2 + core, (y + i) % 4)) for i in range(1, 16)
    ]
    barrier = pltpu.get_barrier_semaphore()
    for _, to in line_to + plane_to:
        pl.semaphore_signal(barrier, inc=1, device_id=to, device_id_type=MESH)

    sub16 = lax.broadcasted_iota(jnp.int32, (16, 128), 0)
    lan16 = lax.broadcasted_iota(jnp.int32, (16, 128), 1)
    line = jnp.zeros((8, 128), F32)
    for a in range(6):
        here_a = jnp.broadcast_to(mask[a].astype(F32), (8, 16)).astype(BF16)
        spread = jnp.where(lan16 == sub16 + a * 16, 1.0, 0.0).astype(BF16)
        line = line + jnp.dot(here_a, spread, preferred_element_type=F32)
    sub8 = lax.broadcasted_iota(jnp.int32, (8, 128), 0)
    mown[...] = jnp.where(sub8 == x * 2 + core, line, 0.0)
    load_group(0)
    pl.semaphore_wait(barrier, 22)
    copies = [remote(mown, mx.at[i - 1], m_ssem.at[i], m_rsem.at[i], to) for i, to in line_to]
    for c in copies:
        c.start()
    load_group(1)
    for c in copies:
        c.wait()
    gathered = mown[...]
    for i in range(7):
        gathered = gathered + mx[i]
    mfour[...] = gathered
    my[pl.ds(y, 1), pl.ds(z, 1)] = gathered.reshape(1, 1, 8, 128)
    for i, to in plane_to:
        remote(mfour, my.at[y, z], m_ssem.at[7 + i], m_rsem.at[7 + i], to).start()
    for g in range(2, N_GROUPS):
        load_group(g)
    front_in.start()
    for i, to in plane_to:
        at = my.at[(y + 16 - i) % 4, (z + 4 - i // 4) % 4]
        remote(mfour, at, m_ssem.at[7 + i], m_rsem.at[7 + i], to).wait()
    masks = my[...].reshape(128, 128).astype(BF16)

    sub = lax.broadcasted_iota(jnp.int32, (SLOTS, SLOTS), 0)
    lan = lax.broadcasted_iota(jnp.int32, (SLOTS, SLOTS), 1)
    eye = sub == lan
    sub_f = sub.astype(F32)

    def to_col(line):
        values = jnp.where(eye, line.astype(F32), 0.0)
        return jnp.sum(values, axis=1, keepdims=True).astype(jnp.int32)

    own = to_col(owner[...])
    at = to_col(slot[...])
    e = (own & 3) * 32 + ((own >> 3) & 3) * 8 + ((own >> 5) & 3) * 2 + ((own >> 2) & 1)
    lanes = lax.broadcasted_iota(jnp.int32, (SLOTS, 128), 1)
    by_owner = jnp.where(e == lanes, 1.0, 0.0).astype(BF16)
    keeps = jnp.dot(by_owner, masks, preferred_element_type=F32)
    keep = jnp.sum(jnp.where(at == lanes, keeps, 0.0), axis=1, keepdims=True)
    keep = jnp.where((at & 15) == 0, 1.0, keep)
    code = jnp.where(keep > 0.5, (e * 128 + at).astype(F32), -1.0)

    def to_row(col):
        return jnp.sum(jnp.where(eye, col, 0.0), axis=0, keepdims=True)

    def axis_shift(m, axis):
        digit = (m.astype(jnp.int32) >> (8, 10, 12)[axis]) & 3
        return ((digit + 4 - here[axis]) & 3).astype(F32)

    def route(col, axis):
        line = to_row(col)
        twin = jnp.max(jnp.where((col == line) & (sub < lan), 1.0, 0.0), axis=0, keepdims=True)
        first = (line >= 0.0) & (twin < 0.5)
        shift_col, shift_line = axis_shift(col, axis), axis_shift(line, axis)
        ahead = first & (shift_line == shift_col) & (line < col)
        rank = jnp.sum(jnp.where(ahead, 1.0, 0.0), axis=1, keepdims=True)
        place = jnp.where((col >= 0.0) & (rank < CAP), shift_col * CAP + rank, -1.0)
        over = jnp.max(jnp.where((col >= 0.0) & (rank >= CAP), 1.0, 0.0), axis=0, keepdims=True)
        goes = sub_f == to_row(place)
        passed = jnp.max(jnp.where(goes, line, -1.0), axis=1, keepdims=True)
        return jnp.where(goes, 1.0, 0.0).astype(BF16), passed, over

    def send_header(phase, p, passed):
        hsend[phase, p] = jnp.broadcast_to(passed, (SLOTS, 128))
        for s in (1, 2, 3):
            remote(
                hsend.at[phase, p, pl.ds(s * CAP, CAP)],
                hrecv.at[phase, p, pl.ds((s - 1) * CAP, CAP)],
                h_ssem.at[phase, p],
                h_rsem.at[phase, p],
                peer(AXES[p][phase], s),
            ).start()

    def take_header(phase, p):
        remote(
            hsend.at[phase, p, pl.ds(CAP, 3 * CAP)],
            hrecv.at[phase, p],
            h_ssem.at[phase, p],
            h_rsem.at[phase, p],
            peer(AXES[p][phase], 1),
        ).wait()
        return jnp.concatenate([hsend[phase, p, 0:CAP, 0:1], hrecv[phase, p, :, 0:1]], axis=0)

    overs = []

    def first_table(p):
        table, passed, over = route(code, AXES[p][0])
        tabs[0, p] = table
        overs.append(over)
        send_header(0, p, passed)

    def later_tables(phase):
        for p in range(3):
            table, passed, over = route(take_header(phase - 1, p), AXES[p][phase])
            tabs[phase, p] = table
            overs.append(over)
            send_header(phase, p, passed)

    def last_tables():
        for p in range(3):
            col = take_header(2, p)
            whole = col.astype(jnp.int32)
            block = (whole & 127) + jnp.where(((whole >> 7) & 1) == core, 96, 0)
            block = jnp.where(col >= 0.0, block.astype(F32), -1.0)
            tabs[3, p] = jnp.where(sub_f == to_row(block), 1.0, 0.0).astype(BF16)

    def split_dot(table, values):
        high = values.astype(BF16)
        low = (values - high.astype(F32)).astype(BF16)
        return jnp.dot(table, high, preferred_element_type=F32) + jnp.dot(
            table, low, preferred_element_type=F32
        )

    recvs = (None, recv1, recv2, recv3)

    def rows_of(phase, i):
        if phase == 0:
            return buf[i]
        return jnp.concatenate([buf[i, 0:CAP, :], recvs[phase][i]], axis=0)

    def chunk_wait(phase, n, r0, rows):
        if phase == 0:
            g, p = CHUNKS[n][:2]
            if p == 0:
                ref = buf.at[pl.ds(SPANS[g][0], SPANS[g][1])]
                pltpu.make_async_copy(ref, ref, child_sem.at[g]).wait()
        else:
            ref = recvs[phase].at[pl.ds(r0, rows)]
            remote(ref, ref, send_sem.at[phase - 1, n], recv_sem.at[phase - 1, n], sibling).wait_recv()

    def forward(phase, n):
        _, p, r0, rows = CHUNKS[n]
        chunk_wait(phase, n, r0, rows)
        table = tabs[phase, p]

        def body(it, carry):
            i = r0 + it * 2
            both = jnp.concatenate([rows_of(phase, i), rows_of(phase, i + 1)], axis=1)
            got = split_dot(table, both)
            for k in range(2):
                part = got[:, k * 128:(k + 1) * 128]
                if phase == 0:
                    buf[i + k] = part
                else:
                    buf[i + k, 0:CAP, :] = part[0:CAP]
                    recvs[phase][i + k] = part[CAP:]
            return carry

        lax.fori_loop(0, rows // 2, body, 0)
        for s in (1, 2, 3):
            if phase == 0:
                src = buf.at[pl.ds(r0, rows), pl.ds(s * CAP, CAP), :]
            else:
                src = recvs[phase].at[pl.ds(r0, rows), pl.ds((s - 1) * CAP, CAP), :]
            remote(
                src,
                recvs[phase + 1].at[pl.ds(r0, rows), pl.ds((s - 1) * CAP, CAP), :],
                send_sem.at[phase, n],
                recv_sem.at[phase, n],
                peer(AXES[p][phase], s),
            ).start()

    def finish(n):
        _, p, r0, rows = CHUNKS[n]
        chunk_wait(3, n, r0, rows)
        table = tabs[3, p]

        def body(it, carry):
            i = r0 + it * 2
            both = jnp.concatenate([rows_of(3, i), rows_of(3, i + 1)], axis=1)
            got = split_dot(table, both)
            for k in range(2):
                part = got[:, k * 128:(k + 1) * 128]
                recv3[i + k, 0:96, :] = part[0:96]
                for a in range(6):
                    fbuf[a, i + k] = fbuf[a, i + k] + part[96 + a * 16:112 + a * 16]
            return carry

        lax.fori_loop(0, rows // 2, body, 0)
        remote(
            recv3.at[pl.ds(r0, rows), pl.ds(0, 96), :],
            sib.at[pl.ds(r0, rows)],
            sib_ssem.at[n],
            sib_rsem.at[n],
            sibling,
        ).start()

    def from_sibling(n):
        _, p, r0, rows = CHUNKS[n]
        ref = sib.at[pl.ds(r0, rows)]
        remote(ref, ref, sib_ssem.at[n], sib_rsem.at[n], sibling).wait_recv()

        def body(it, carry):
            i = r0 + it
            got = sib[i]
            for a in range(6):
                fbuf[a, i] = fbuf[a, i] + got[a * 16:a * 16 + 16]
            return carry

        lax.fori_loop(0, rows, body, 0)
        pltpu.make_async_copy(
            fbuf.at[:, pl.ds(r0, rows)], out.at[:, pl.ds(r0, rows)], out_sem.at[n]
        ).start()

    holds = core == y % 2
    on_line = z % 2 == y // 2
    mine = 2 * x + z // 2
    other = 2 * x + ((z + 2) % 4) // 2
    lower = 2 * x
    source = jnp.logical_and(holds, on_line)
    off_line = jnp.logical_and(holds, jnp.logical_not(on_line))

    def pan_copy(g):
        r0, rows = SPANS[g]
        return pltpu.make_async_copy(
            pan.at[:, pl.ds(r0, rows)], panel.at[y, :, pl.ds(r0, rows)], pan_sem.at[g]
        )

    def y_copy(g, s, at):
        r0, rows = SPANS[g]
        return remote(
            pan.at[:, pl.ds(r0, rows)], panel.at[at, :, pl.ds(r0, rows)],
            y_ssem.at[g, s - 1], y_rsem.at[g, s - 1], peer(2, s),
        )

    def panel_out(g):
        r0, rows = SPANS[g]

        def body(it, carry):
            i = pl.multiple_of(r0 + it * 4, 4)
            for a in range(6):
                for k in range(4):
                    pan[a, pl.ds(i + k, 1), :] = fbuf[a, i + k, 0:1, :]
            return carry

        lax.fori_loop(0, rows // 4, body, 0)
        pan_copy(g).start()
        for s in (1, 2, 3):
            y_copy(g, s, y).start()

    def trail_at(g, place, half):
        r0, rows = SPANS[g]
        return trail.at[place, :, half, pl.ds(r0, rows)]

    def source_copy(g, half, sems, s, place):
        r0, rows = SPANS[g]
        return remote(
            panel.at[:, half, pl.ds(r0, rows)], trail_at(g, place, half),
            sems[0].at[g, 0, s - 1], sems[1].at[g, 0, s - 1], peer(half, s),
        )

    def own_copy(g, half):
        r0, rows = SPANS[g]
        return pltpu.make_async_copy(
            panel.at[:, half, pl.ds(r0, rows)], trail_at(g, mine, half), pan_sem.at[N_GROUPS + half * N_GROUPS + g]
        )

    a_sems, b_sems = (a_ssem, a_rsem), (b_ssem, b_rsem)

    def from_x(s):
        return 2 * ((x + 4 - s) % 4)

    def panel_rows(g):
        pan_copy(g).wait()
        for s in (1, 2, 3):
            y_copy(g, s, (y + 4 - s) % 4).wait_recv()

        @pl.when(source)
        def _():
            for half in (0, 1):
                own_copy(g, half).start()
                for s in (1, 2, 3):
                    source_copy(g, half, (a_sems, b_sems)[half], s, mine).start()

    def a_line(g, s, i, base):
        place = 2 * i + base // 2
        ref = trail_at(g, place, 0)
        return remote(ref, ref, a_ssem.at[g, 1 + i, s - 1], a_rsem.at[g, 1 + i, s - 1], peer(1, s))

    def b_line(g, s, zz, at):
        ref = trail_at(g, 2 * at + zz, 1)
        return remote(ref, ref, b_ssem.at[g, 1 + zz, s - 1], b_rsem.at[g, 1 + zz, s - 1], peer(0, s))

    def relayed(g):
        return g < N_GROUPS - 2

    def relay(g, i, base):
        place = 2 * i + base // 2
        ref = trail_at(g, place, 0)
        return remote(ref, ref, a_ssem.at[g, 1 + i, 1], a_rsem.at[g, 1 + i, 1], peer(1, 1 if i < 2 else 3))

    def panel_lines(g):
        @pl.when(source)
        def _():
            for half in (0, 1):
                own_copy(g, half).wait()
            for s in (1, 2, 3):
                source_copy(g, 0, a_sems, s, from_x(s) + z // 2).wait_recv()
            for i in range(4):
                for s in (1, 3) if relayed(g) else (1, 3, 2):
                    a_line(g, s, i, z).start()
            source_copy(g, 1, b_sems, 2, other).wait_recv()

        @pl.when(off_line)
        def _():
            for s in (1, 3):
                source_copy(g, 1, b_sems, s, lower + ((z + 4 - s) % 4) // 2).wait_recv()

        @pl.when(holds)
        def _():
            for zz in (0, 1):
                for s in (1, 2, 3):
                    b_line(g, s, zz, x).start()

    def to_sibling(g):
        r0, rows = SPANS[g]
        ref = trail.at[:, :, :, pl.ds(r0, rows)]
        return remote(ref, ref, c_ssem.at[g], c_rsem.at[g], sibling)

    def panel_cores(g):
        @pl.when(off_line)
        def _():
            for i in range(4):
                for s in (1, 3):
                    a_line(g, s, i, (z + 4 - s) % 4).wait_recv()
            if relayed(g):
                for i in range(4):
                    relay(g, i, (z + 3) % 4 if i < 2 else (z + 1) % 4).start()

        @pl.when(holds)
        def _():
            for zz in (0, 1):
                for s in (1, 2, 3):
                    b_line(g, s, zz, (x + 4 - s) % 4).wait_recv()

    def panel_ends(g):
        @pl.when(source)
        def _():
            for i in range(4):
                a_line(g, 2, i, (z + 2) % 4).wait_recv()

        @pl.when(holds)
        def _():
            to_sibling(g).start()

    def panel_end(g):
        for s in (1, 2, 3):
            y_copy(g, s, y).wait_send()

        @pl.when(source)
        def _():
            for half in (0, 1):
                for s in (1, 2, 3):
                    source_copy(g, half, (a_sems, b_sems)[half], s, mine).wait_send()
            for i in range(4):
                for s in (1, 3) if relayed(g) else (1, 2, 3):
                    a_line(g, s, i, z).wait_send()

        if relayed(g):

            @pl.when(off_line)
            def _():
                for i in range(4):
                    relay(g, i, (z + 3) % 4 if i < 2 else (z + 1) % 4).wait_send()

        @pl.when(holds)
        def _():
            for zz in (0, 1):
                for s in (1, 2, 3):
                    b_line(g, s, zz, x).wait_send()
            to_sibling(g).wait_send()

        @pl.when(jnp.logical_not(holds))
        def _():
            to_sibling(g).wait_recv()

    def flag_copies(step):
        return [
            remote(fsend.at[step], frecv.at[step, s - 1], f_ssem.at[step, s - 1],
                   f_rsem.at[step, s - 1], peer(step, s))
            for s in (1, 2, 3)
        ]

    flag_last = remote(fsend.at[3], frecv.at[3, 0], f_ssem.at[3, 0], f_rsem.at[3, 0], sibling)

    def flag_step(step):
        if step > 0:
            for c in flag_copies(step - 1):
                c.wait()
            fsend[step] = (
                fsend[step - 1] + frecv[step - 1, 0] + frecv[step - 1, 1] + frecv[step - 1, 2]
            )
        for c in flag_copies(step) if step < 3 else [flag_last]:
            c.start()

    flags_done = 0
    steps = sorted((stage + g, stage, g) for stage in range(9) for g in range(N_GROUPS))
    for _, stage, g in steps:
        chunks = [n for n in range(N_CHUNKS) if CHUNKS[n][0] == g]
        if stage < 3:
            if g == 0 and stage > 0:
                later_tables(stage)
            for n in chunks:
                if stage == 0 and g == 0:
                    first_table(CHUNKS[n][1])
                forward(stage, n)
        elif stage == 3:
            if g == 0:
                last_tables()
                total = overs[0]
                for o in overs[1:]:
                    total = jnp.maximum(total, o)
                fsend[0] = jnp.broadcast_to(total, (8, 128))
                front_in.wait()
            for n in chunks:
                finish(n)
        elif stage == 4:
            for n in chunks:
                from_sibling(n)
            panel_out(g)
        elif stage == 5:
            panel_rows(g)
        elif stage == 6:
            panel_lines(g)
        elif stage == 7:
            panel_cores(g)
        else:
            panel_ends(g)
        if stage >= 3 and flags_done < 4:
            flag_step(flags_done)
            flags_done += 1
    flag_last.wait()
    flag[0, 0] = jnp.max(fsend[3] + frecv[3, 0]).astype(jnp.int32)
    for n, (_, _, r0, rows) in enumerate(CHUNKS):
        for phase in range(3):
            ref = recvs[phase + 1].at[pl.ds(r0, rows)]
            remote(ref, ref, send_sem.at[phase, n], recv_sem.at[phase, n], sibling).wait_send()
        ref = sib.at[pl.ds(r0, rows)]
        remote(ref, ref, sib_ssem.at[n], sib_rsem.at[n], sibling).wait_send()
        pltpu.make_async_copy(
            fbuf.at[:, pl.ds(r0, rows)], out.at[:, pl.ds(r0, rows)], out_sem.at[n]
        ).wait()
    for g in range(N_GROUPS):
        panel_end(g)


def exchange(child, front, owner, slot, mask):
    dma = pltpu.SemaphoreType.DMA
    vmem = pl.BlockSpec(memory_space=pltpu.VMEM)
    hbm = pl.BlockSpec(memory_space=pl.ANY)
    return pl.pallas_call(
        exchange_kernel,
        out_shape=(
            jax.ShapeDtypeStruct((6, 128, 16, 128), F32),
            jax.ShapeDtypeStruct((4, 6, 128, 128), F32),
            jax.ShapeDtypeStruct((8, 4, 2, 128, 128), F32),
            jax.ShapeDtypeStruct((1, 1), jnp.int32),
        ),
        in_specs=[hbm, hbm, vmem, vmem, vmem],
        out_specs=(hbm, hbm, hbm, pl.BlockSpec(memory_space=pltpu.SMEM)),
        scratch_shapes=[
            pltpu.VMEM((128, SLOTS, 128), F32),
            pltpu.VMEM((128, 3 * CAP, 128), F32),
            pltpu.VMEM((128, 3 * CAP, 128), F32),
            pltpu.VMEM((128, 3 * CAP, 128), F32),
            pltpu.VMEM((128, 96, 128), F32),
            pltpu.VMEM((6, 128, 16, 128), F32),
            pltpu.VMEM((6, 128, 128), F32),
            pltpu.VMEM((4, 3, SLOTS, SLOTS), BF16),
            pltpu.VMEM((8, 128), F32),
            pltpu.VMEM((7, 8, 128), F32),
            pltpu.VMEM((8, 128), F32),
            pltpu.VMEM((4, 4, 8, 128), F32),
            pltpu.VMEM((3, 3, SLOTS, 128), F32),
            pltpu.VMEM((3, 3, 3 * CAP, 128), F32),
            pltpu.VMEM((4, 8, 128), F32),
            pltpu.VMEM((4, 3, 8, 128), F32),
            dma((N_GROUPS,)),
            dma,
            dma((N_CHUNKS,)),
            dma((3, N_CHUNKS)),
            dma((3, N_CHUNKS)),
            dma((N_CHUNKS,)),
            dma((N_CHUNKS,)),
            dma((23,)),
            dma((23,)),
            dma((3, 3)),
            dma((3, 3)),
            dma((4, 3)),
            dma((4, 3)),
            dma((3 * N_GROUPS,)),
            dma((N_GROUPS, 3)),
            dma((N_GROUPS, 3)),
            dma((N_GROUPS, 5, 3)),
            dma((N_GROUPS, 5, 3)),
            dma((N_GROUPS, 3, 3)),
            dma((N_GROUPS, 3, 3)),
            dma((N_GROUPS,)),
            dma((N_GROUPS,)),
        ],
        compiler_params=pltpu.CompilerParams(
            collective_id=0, has_side_effects=True, vmem_limit_bytes=62 * 2**20
        ),
        name="tile_exchange",
    )(child, front, owner, slot, mask)


def schur_kernel(
    col_at, mask, order, inverse, panel, trail, front, out,
    n_high, n_low, m_high, m_low, t_high, t_low,
):
    def split(values):
        high = values.astype(BF16)
        return high, (values - high.astype(F32)).astype(BF16)

    def dot(a, b):
        return jnp.dot(a, b, preferred_element_type=F32)

    def dot_t(a, b):
        return lax.dot_general(a, b, (((1,), (1,)), ((), ())), preferred_element_type=F32)

    def three(left, right, how):
        return how(left[0], right[0]) + how(left[0], right[1]) + how(left[1], right[0])

    @pl.when(pl.program_id(0) == 0)
    def _():
        sub = lax.broadcasted_iota(jnp.int32, (512, 512), 0)
        place = jnp.where(sub == order[...], 1.0, 0.0).astype(BF16)
        for part, n_ref, m_ref in zip(split(inverse[...]), (n_high, n_low), (m_high, m_low)):
            rows = dot(place, part).astype(BF16)
            n_ref[...] = rows
            m_ref[...] = dot_t(rows, place).astype(BF16)
        for half in range(2):
            for m in range(8):
                for k in range(4):
                    high, low = split(trail[m, k, half])
                    t_high[half * 8 + m, :, k * 128:(k + 1) * 128] = high
                    t_low[half * 8 + m, :, k * 128:(k + 1) * 128] = low

    pair = pl.program_id(0)
    rows = jnp.concatenate(
        [jnp.concatenate([panel[k, a] for k in range(4)], axis=1) for a in range(2)], axis=0
    )
    rows = split(rows)
    mine = pl.ds(pl.multiple_of(col_at[0] * 128, 128), 128)
    factor = three(rows, (n_high[:, mine], n_low[:, mine]), dot)
    turned = split(three(rows, (m_high[...], m_low[...]), dot))
    for a in range(2):
        out[pl.ds(a * 2048, 128, stride=16), :] = factor[a * 128:(a + 1) * 128]
    for first in range(0, 16, 2):
        cols = (
            t_high[first:first + 2].reshape(256, 512),
            t_low[first:first + 2].reshape(256, 512),
        )
        update = three(turned, cols, dot_t)
        for b in (first, first + 1):
            if b == 0:
                continue
            for a in range(2):
                at = pl.ds(a * 2048 + b, 128, stride=16)
                part = update[a * 128:(a + 1) * 128, (b - first) * 128:(b - first + 1) * 128]
                keep = mask[pair * 2 + a, b] > 0
                out[at, :] = jnp.where(keep, front[at, :] - part, 0.0)


def finish_front(col_at, mask, order, inverse, panel, trail, assembled):
    smem = pl.BlockSpec(memory_space=pltpu.SMEM)
    return pl.pallas_call(
        schur_kernel,
        grid=(3,),
        out_shape=jax.ShapeDtypeStruct((12288, 128), F32),
        in_specs=[
            smem,
            smem,
            pl.BlockSpec((1, 512), lambda i: (0, 0)),
            pl.BlockSpec((512, 512), lambda i: (0, 0)),
            pl.BlockSpec((4, 2, 128, 128), lambda i: (0, i, 0, 0)),
            pl.BlockSpec((8, 4, 2, 128, 128), lambda i: (0, 0, 0, 0, 0)),
            pl.BlockSpec((4096, 128), lambda i: (i, 0)),
        ],
        out_specs=pl.BlockSpec((4096, 128), lambda i: (i, 0)),
        scratch_shapes=[
            pltpu.VMEM((512, 512), BF16),
            pltpu.VMEM((512, 512), BF16),
            pltpu.VMEM((512, 512), BF16),
            pltpu.VMEM((512, 512), BF16),
            pltpu.VMEM((16, 128, 512), BF16),
            pltpu.VMEM((16, 128, 512), BF16),
        ],
        compiler_params=pltpu.CompilerParams(vmem_limit_bytes=40 * 2**20),
        name="schur",
    )(col_at, mask, order, inverse, panel, trail, assembled)


def any_front(front, mask, child_tiles, owner_map, parent_slot, pivot_order, inv_pivot):
    n_row = lax.axis_size("row")
    n_col = lax.axis_size("col")
    devices = n_row * n_col
    blk_rows = front.shape[0]
    block_size = front.shape[2]
    blk_cols = front.shape[3]
    rows_here = blk_rows * block_size
    local_width = blk_cols * block_size
    panel_size = inv_pivot.shape[0]
    panel_local = panel_size // (block_size * n_col)
    slots_total = blk_rows * blk_cols
    tile_area = child_tiles.shape[1]
    owner_dev = owner_map[:, 0]
    owner_hits = (owner_dev[:, None] == jnp.arange(devices, dtype=jnp.int32)[None, :]).astype(
        jnp.int32
    )
    earlier = jnp.cumsum(owner_hits, axis=0) - owner_hits
    tile_rank = jnp.sum(earlier * owner_hits, axis=1)
    send_slot = owner_dev * MOST + tile_rank
    outgoing = jnp.zeros((devices * MOST, tile_area), jnp.float32).at[send_slot].set(child_tiles)
    targets = jnp.full((devices * MOST,), slots_total, jnp.int32).at[send_slot].set(parent_slot)
    arrived, places = (
        lax.all_to_all(
            outgoing.reshape(devices, MOST, tile_area),
            ("row", "col"),
            split_axis=0,
            concat_axis=0,
            tiled=True,
        ),
        lax.all_to_all(
            targets.reshape(devices, MOST), ("row", "col"), split_axis=0, concat_axis=0, tiled=True
        ),
    )
    arrived = arrived.reshape(devices * MOST, tile_area)
    places = places.reshape(devices * MOST)
    blocks = jnp.zeros((slots_total, tile_area), jnp.float32).at[places].add(arrived, mode="drop")
    contrib = (
        blocks.reshape(blk_rows, blk_cols, block_size, block_size)
        .transpose(0, 2, 1, 3)
        .reshape(rows_here, local_width)
    )
    assembled = front.reshape(rows_here, local_width) + contrib
    own_panel = assembled[:, : panel_local * block_size]
    gathered = lax.all_gather(own_panel, "col", axis=1, tiled=True)
    panel_cols = (
        gathered.reshape(rows_here, n_col, panel_local, block_size)
        .transpose(0, 2, 1, 3)
        .reshape(rows_here, panel_size)
    )
    permuted = jnp.take(panel_cols, pivot_order, axis=1)
    factor = jnp.dot(permuted, inv_pivot, precision=lax.Precision.HIGHEST)
    col_here = lax.axis_index("col")
    window_local = blk_cols * n_col // n_row
    window_mine = permuted[: window_local * block_size]
    everything = lax.all_gather(window_mine, "row", axis=0, tiled=True).reshape(
        n_row, window_local, block_size, panel_size
    )
    block_index = jnp.arange(blk_cols, dtype=jnp.int32) * n_col + col_here
    needed = everything[block_index % n_row, block_index // n_row]
    needed = needed.reshape(blk_cols * block_size, panel_size)
    trailing = needed[panel_local * block_size :]
    update = jnp.einsum("rp,cp->rc", factor, trailing, precision=lax.Precision.HIGHEST)
    keep_block = mask.reshape(blk_rows, blk_cols)[:, panel_local:] > 0
    schur_part = (assembled[:, panel_local * block_size :] - update).reshape(
        blk_rows, block_size, blk_cols - panel_local, block_size
    )
    schur_part = jnp.where(keep_block[:, None, :, None], schur_part, 0.0)
    factor_mine = lax.dynamic_slice_in_dim(
        factor.reshape(rows_here, panel_local, n_col, block_size), col_here, 1, 2
    ).reshape(rows_here, panel_local * block_size)
    result = jnp.concatenate(
        [factor_mine, schur_part.reshape(rows_here, (blk_cols - panel_local) * block_size)], 1
    )
    return result.reshape(front.shape)


def per_device(front, mask, child_tiles, owner_map, parent_slot, pivot_order, inv_pivot):
    child4 = child_tiles.reshape(24, 8, 128, 128).transpose(0, 2, 1, 3)
    mask_here = mask.reshape(6, 16)
    assembled, panel, trail, flag = exchange(
        child4,
        front.reshape(6, 128, 16, 128),
        owner_map.reshape(1, 192),
        parent_slot.reshape(1, 192),
        mask.reshape(6, 1, 16),
    )
    col_at = lax.axis_index("col").astype(jnp.int32).reshape(1)
    return lax.cond(
        flag[0, 0] > 0,
        lambda: any_front(
            front, mask, child_tiles, owner_map, parent_slot, pivot_order, inv_pivot
        ),
        lambda: finish_front(
            col_at,
            mask_here,
            pivot_order.reshape(1, 512),
            inv_pivot,
            panel,
            trail,
            assembled.reshape(12288, 128),
        ).reshape(front.shape),
    )


def solution(mesh):
    placed = (
        P(None, "row", None, None, "col", None),
        P(None, "row", None, "col"),
        P(("row", "col"), None),
        P(("row", "col"), None),
        P(("row", "col")),
        P(),
        P(),
    )
    return jax.shard_map(
        per_device,
        mesh=mesh,
        in_specs=placed,
        out_specs=P(None, "row", None, None, "col", None),
        check_vma=False,
    )
```
